512 devices in a mesh: row: 32 (over x, z_lo), ch: 16 (over y, z_hi, core).
Axes of the slice: x: 4, y: 4, z: 16 (z_hi: 2, z_lo: 8; z = z_hi * 8 + z_lo), core: 2. Of those that a mesh axis runs over, the one named last changes fastest.
Arguments:
- pair: float32 [256, 256, 128], P('row', 'ch'), may hold values from -6 to 6
- pair_mask: int32 [256, 256], P('row', 'ch'), may hold values 0 or 1
- w_in: float32 [128, 512], replicated, may hold values from -0.5 to 0.5
- w_gate: float32 [128, 128], replicated, may hold values from -0.5 to 0.5
- w_out: float32 [128, 128], replicated, may hold values from -0.5 to 0.5
- cotangent: float32 [256, 256, 128], P('row', 'ch'), may hold values from -6 to 6
Outputs:
- update: float32 [256, 256, 128], P('row', 'ch')
- d_pair: float32 [256, 256, 128], P('row', 'ch')
- d_w_in: float32 [128, 512], replicated
- d_w_gate: float32 [128, 128], replicated
- d_w_out: float32 [128, 128], replicated
The draws below stay inside these ranges and needn't reach their ends.
All inputs are finite; a program needn't handle non-finite values. No bound on the sum of `pair_mask` on one device may be relied on, other than what follows from the above.
Results may differ from the reference program's by a relative error of at most 0.00014.
Values sent between devices are 32-bit elements; how exact they have to be, the bound alone decides.
No kernel may reach another device: no remote copies, remote signals or barrier semaphores. Data moves between devices by JAX's collectives and lax.ppermute only.
A program may use at most 64 MiB of HBM per device.

```python
import jax
import jax.numpy as jnp
from jax import lax

C = 128
H = 128
N = 256


def touch_ends(result, stream_key, low, top_value):
    extent = result.shape
    index_at = [jax.random.randint(jax.random.fold_in(stream_key, axis), (), 0, extent[axis]) for axis in range(len(extent))]
    result = result.at[tuple(index_at)].set(low)
    longest = extent.index(max(extent))
    index_at[longest] = (index_at[longest] + 1) % extent[longest]
    return result.at[tuple(index_at)].set(top_value)


def levels(stream_key, extent, shards, smallest, high):
    def one(dim, parts):
        draws = jax.random.uniform(jax.random.fold_in(jax.random.fold_in(stream_key, 6), dim), (parts,), jnp.float32, smallest / len(shards), high / len(shards))
        return jnp.repeat(jnp.exp(draws), extent[dim] // parts).reshape((-1,) + (1,) * (len(extent) - dim - 1))

    level = one(*shards[0])
    for cut in shards[1:]:
        level = level * one(*cut)
    return level


def gaussian(stream_key, dims, deviation, bound, pieces=(), kind=jnp.bfloat16):
    level = levels(stream_key, dims, pieces, -0.22, 0.18) if pieces else 1.0
    result = jax.random.normal(stream_key, dims, jnp.float32) * deviation * level
    return jnp.minimum(jnp.maximum(result, -bound), bound).astype(kind)


def setup_inputs(seed: int = 0) -> dict:
    key_list = jax.random.split(jax.random.key(seed), 7)
    pair = gaussian(key_list[0], (N, N, C), 1.0, 6.0, ((0, 32), (1, 16)), jnp.float32)
    pair_mask = touch_ends((jax.random.randint(key_list[1], (N, N), 0, 8) < 7).astype(jnp.int32), jax.random.fold_in(key_list[1], 1), 0, 1)
    w_in = gaussian(key_list[2], (C, 4 * H), C ** -0.5, 0.5, (), jnp.float32)
    w_gate = gaussian(key_list[3], (C, C), C ** -0.5, 0.5, (), jnp.float32)
    w_out = gaussian(key_list[4], (H, C), H ** -0.5, 0.5, (), jnp.float32)
    cotangent = gaussian(key_list[5], (N, N, C), 1.0, 6.0, ((0, 32), (1, 16)), jnp.float32)
    return {"pair": pair, "pair_mask": pair_mask, "w_in": w_in, "w_gate": w_gate, "w_out": w_out, "cotangent": cotangent}


def layer_norm(values):
    center = values - lax.optimization_barrier(jnp.mean(values, axis=-1, keepdims=True))
    spread = lax.optimization_barrier(jnp.mean(center * center, axis=-1, keepdims=True))
    return center / jnp.sqrt(spread + 1e-05)

def forward(pair, w_in, w_gate, w_out, pair_mask):
    highest = lax.Precision.HIGHEST
    normed_pair = layer_norm(pair)
    projected = jnp.einsum('ikc,cf->ikf', normed_pair, w_in, precision=highest)
    maskf = pair_mask.astype(jnp.float32)[:, :, None]
    left = maskf * jax.nn.sigmoid(projected[:, :, :H]) * projected[:, :, H:2 * H]
    right = maskf * jax.nn.sigmoid(projected[:, :, 2 * H:3 * H]) * projected[:, :, 3 * H:]
    gate = jax.nn.sigmoid(jnp.einsum('ikc,cd->ikd', normed_pair, w_gate, precision=highest))
    triangle = jnp.einsum('ikh,jkh->ijh', left, right, precision=highest)
    normed_tri = layer_norm(triangle)
    return gate * jnp.einsum('ijh,hc->ijc', normed_tri, w_out, precision=highest)

def reference(pair, pair_mask, w_in, w_gate, w_out, cotangent):

    def apply(pair_in, win_in, wgate_in, wout_in):
        return forward(pair_in, win_in, wgate_in, wout_in, pair_mask)
    update, pullback = jax.vjp(apply, pair, w_in, w_gate, w_out)
    d_pair, d_w_in, d_w_gate, d_w_out = pullback(cotangent)
    return (update, d_pair, d_w_in / N, d_w_gate / N, d_w_out / N)
```

```python
import jax
import jax.numpy as jnp
from jax import lax
from jax.experimental import pallas as pl
from jax.experimental.pallas import tpu as pltpu
from jax.sharding import Mesh, PartitionSpec as P

ROW = ("x", "zl")
CH = ("y", "zh", "co")
CHANNELS = ("zh", "co", "x", "zl")
PLANE = ("x", "y", "co")
DEPTH = ("zl", "zh")
F32 = jnp.float32
EPS = 1e-05


def dot(a, b, ca, cb):
    return lax.dot_general(
        a, b, (((ca,), (cb,)), ((), ())), precision=lax.Precision.HIGHEST, preferred_element_type=F32
    )


def call(body, outs, scratch=()):
    vmem = pl.BlockSpec(memory_space=pltpu.VMEM)

    def run(*args):
        return pl.pallas_call(
            body,
            out_shape=[jax.ShapeDtypeStruct(s, F32) for s in outs],
            in_specs=[vmem] * len(args),
            out_specs=[vmem] * len(outs),
            scratch_shapes=[pltpu.VMEM(s, F32) for s in scratch],
            compiler_params=pltpu.CompilerParams(vmem_limit_bytes=32 * 1024 * 1024),
        )(*args)

    return run


def norm_rows(values):
    center = values - jnp.mean(values, axis=1, keepdims=True)
    spread = jnp.mean(center * center, axis=1, keepdims=True)
    rstd = 1.0 / jnp.sqrt(spread + EPS)
    return center * rstd, rstd


def mask_lanes(mask_ref, lanes_ref):
    maskf = mask_ref[...].astype(F32)
    for ii in range(8):
        lanes_ref[0:1, ii * 16 : (ii + 1) * 16] = maskf[ii : ii + 1, :]
    return lanes_ref[0:1, :]


def enter_kernel(pair_ref, mask_ref, win_ref, wgate_ref, msg_ref, proj_ref, normed_ref, gate_ref, lanes_ref):
    normed, _ = norm_rows(pair_ref[...].reshape(128, 128))
    maskf = mask_lanes(mask_ref, lanes_ref)
    proj = dot(win_ref[...], normed, 0, 1)
    proj_ref[...] = proj
    msg_ref[:, 0, 0:128] = maskf * jax.nn.sigmoid(proj[0:128]) * proj[128:256]
    msg_ref[:, 0, 128:256] = maskf * jax.nn.sigmoid(proj[256:384]) * proj[384:512]
    normed_ref[...] = normed
    gate_ref[...] = jax.nn.sigmoid(dot(normed, wgate_ref[...], 1, 0))


def triangle_kernel(msg_ref, part_ref, left_ref, right_ref, flat_ref, turn_ref):
    flat_ref[...] = msg_ref[:, 0, :]
    for s in range(8):
        rows = slice(s * 32, (s + 1) * 32)
        for q in range(4):
            block = flat_ref[q * 32 : (q + 1) * 32, s * 16 : (s + 1) * 16]
            left_ref[rows, q * 16 : (q + 1) * 16] = block
            block = flat_ref[q * 32 : (q + 1) * 32, 128 + s * 16 : 128 + (s + 1) * 16]
            turn_ref[rows, q * 16 : (q + 1) * 16] = block
        right_ref[pl.ds(s, 32, stride=8), :] = turn_ref[rows, :]
    part_ref[...] = dot(right_ref[...], left_ref[...], 1, 1).reshape(4, 64, 256)


def home_kernel(part_ref, msg_ref, flat_ref):
    total = ((part_ref[0] + part_ref[1]) + (part_ref[2] + part_ref[3])).T
    for q in range(4):
        for s in range(8):
            flat_ref[q * 32 : (q + 1) * 32, s * 16 : (s + 1) * 16] = total[
                s * 32 : (s + 1) * 32, q * 16 : (q + 1) * 16
            ]
    msg_ref[:, 0, :] = flat_ref[...]


def norm_channels(values):
    center = values - jnp.mean(values, axis=0, keepdims=True)
    spread = jnp.mean(center * center, axis=0, keepdims=True)
    rstd = 1.0 / jnp.sqrt(spread + EPS)
    return center * rstd, rstd


def turn_kernel(tri_ref, cot_ref, gate_ref, wout_ref, msg_ref):
    normed, rstd = norm_channels(tri_ref[:, 0, :])
    d_out = cot_ref[...].reshape(128, 128) * gate_ref[...]
    d_normed = dot(wout_ref[...], d_out, 1, 1)
    along = jnp.mean(d_normed * normed, axis=0, keepdims=True)
    msg_ref[:, 0, :] = rstd * (d_normed - jnp.mean(d_normed, axis=0, keepdims=True) - normed * along)


def update_kernel(tri_ref, cot_ref, gate_ref, normed_ref, wgate_ref, wout_ref, upd_ref, dn_ref, dwg_ref, dwo_ref):
    normed_tri, _ = norm_channels(tri_ref[:, 0, :])
    gate = gate_ref[...]
    cot = cot_ref[...].reshape(128, 128)
    out_proj = dot(normed_tri, wout_ref[...], 0, 0)
    upd_ref[...] = (gate * out_proj).reshape(8, 16, 128)
    dwo_ref[...] = dot(normed_tri, cot * gate, 1, 0)
    d_pre = cot * out_proj * gate * (1.0 - gate)
    dwg_ref[...] = dot(normed_ref[...], d_pre, 0, 0)
    dn_ref[...] = dot(d_pre, wgate_ref[...], 1, 1)


def spread_kernel(msg_ref, out_ref, flat_ref, whole_ref):
    flat_ref[...] = msg_ref[:, 0, :]
    for q in range(4):
        for s in range(8):
            whole_ref[s * 32 : (s + 1) * 32, q * 16 : (q + 1) * 16] = flat_ref[
                q * 32 : (q + 1) * 32, s * 16 : (s + 1) * 16
            ]
    turned = whole_ref[...].T
    for y in range(4):
        out_ref[y] = turned


def back_kernel(dtri_ref, left_ref, right_ref, msg_ref, flat_ref, dright_ref):
    dtri = dtri_ref[...].reshape(256, 256)
    d_left = dot(dtri, right_ref[...], 0, 0)
    dright_ref[...] = dot(dtri, left_ref[...], 1, 0)
    for s in range(8):
        d_right = dright_ref[pl.ds(s, 32, stride=8), :]
        for q in range(4):
            rows, lanes = slice(q * 32, (q + 1) * 32), slice(q * 16, (q + 1) * 16)
            flat_ref[rows, s * 16 : (s + 1) * 16] = d_left[s * 32 : (s + 1) * 32, lanes]
            flat_ref[rows, 128 + s * 16 : 128 + (s + 1) * 16] = d_right[:, lanes]
    msg_ref[:, 0, :] = flat_ref[...]


def leave_kernel(
    msg_ref, proj_ref, pair_ref, mask_ref, win_ref, dn_ref, dwg_ref, dwo_ref, dpair_ref, weights_ref, dproj_ref, lanes_ref
):
    normed, rstd = norm_rows(pair_ref[...].reshape(128, 128))
    maskf = mask_lanes(mask_ref, lanes_ref)
    for side in range(2):
        base = side * 256
        d_side = maskf * msg_ref[:, 0, side * 128 : (side + 1) * 128]
        sig = jax.nn.sigmoid(proj_ref[base : base + 128])
        d_value = d_side * sig
        dproj_ref[base : base + 128] = d_value * proj_ref[base + 128 : base + 256] * (1.0 - sig)
        dproj_ref[base + 128 : base + 256] = d_value
    d_proj = dproj_ref[...]
    weights_ref[0:512] = dot(d_proj, normed, 1, 0)
    weights_ref[512:640] = dwg_ref[...]
    weights_ref[640:768] = dwo_ref[...]
    d_normed = dot(d_proj, win_ref[...], 0, 1) + dn_ref[...]
    along = jnp.mean(d_normed * normed, axis=1, keepdims=True)
    d_pair = rstd * (d_normed - jnp.mean(d_normed, axis=1, keepdims=True) - normed * along)
    dpair_ref[...] = d_pair.reshape(8, 16, 128)


def sum_kernel(scale, parts_ref, out_ref):
    total = jnp.sum(parts_ref[...], axis=0) * scale
    for i in range(out_ref.shape[0]):
        out_ref[i] = total


def unpack_kernel(parts_ref, dwin_ref, dwg_ref, dwo_ref):
    whole = parts_ref[...].reshape(768, 128)
    dwin_ref[...] = whole[0:512].T
    dwg_ref[...] = whole[512:640]
    dwo_ref[...] = whole[640:768]


def swap(values, axes):
    return lax.all_to_all(values, axes, split_axis=0, concat_axis=0, tiled=True)


def shards(pair, pair_mask, w_in, w_gate, w_out, cotangent):
    msg, proj, normed, gate = call(
        enter_kernel, [(128, 1, 256), (512, 128), (128, 128), (128, 128)], [(8, 128)]
    )(pair, pair_mask, w_in, w_gate)
    msg = swap(msg, CHANNELS)
    part, left, right = call(triangle_kernel, [(4, 64, 256), (256, 64), (256, 64)], [(128, 256), (256, 64)])(msg)
    part = swap(part, "y")
    (msg,) = call(home_kernel, [(128, 1, 128)], [(128, 128)])(part)
    tri = swap(msg, CHANNELS)
    (msg,) = call(turn_kernel, [(128, 1, 128)])(tri, cotangent, gate, w_out)
    msg = swap(msg, CHANNELS)
    update, d_normed, d_wgate, d_wout = call(
        update_kernel, [(8, 16, 128), (128, 128), (128, 128), (128, 128)]
    )(tri, cotangent, gate, normed, w_gate, w_out)
    (d_tri,) = call(spread_kernel, [(4, 64, 256)], [(128, 128), (256, 64)])(msg)
    d_tri = swap(d_tri, "y")
    (msg,) = call(back_kernel, [(128, 1, 256)], [(128, 256), (256, 64)])(d_tri, left, right)
    msg = swap(msg, CHANNELS)
    d_pair, weights = call(
        leave_kernel, [(8, 16, 128), (768, 128)], [(512, 128), (8, 128)]
    )(msg, proj, pair, pair_mask, w_in, d_normed, d_wgate, d_wout)
    parts = swap(weights.reshape(32, 24, 128), PLANE)
    (parts,) = call(lambda a, b: sum_kernel(1.0, a, b), [(16, 24, 128)])(parts)
    parts = swap(parts, DEPTH)
    scale = 1.0 / (pair.shape[0] * lax.axis_size(ROW))
    (parts,) = call(lambda a, b: sum_kernel(scale, a, b), [(32, 24, 128)])(parts)
    parts = swap(parts, PLANE)
    d_win, d_wgate, d_wout = call(unpack_kernel, [(128, 512), (128, 128), (128, 128)])(parts)
    return (update, d_pair, d_win, d_wgate, d_wout)


def solution(mesh):
    fine = Mesh(mesh.devices.reshape(4, 8, 4, 2, 2), ("x", "zl", "y", "zh", "co"))
    in_specs = (P(ROW, CH, None), P(ROW, CH), P(), P(), P(), P(ROW, CH, None))
    out_specs = (P(ROW, CH, None), P(ROW, CH, None), P(), P(), P())
    return jax.shard_map(shards, mesh=fine, in_specs=in_specs, out_specs=out_specs, check_vma=False)
```

```python
import jax
import jax.numpy as jnp
from jax import lax
from jax.experimental import pallas as pl
from jax.experimental.pallas import tpu as pltpu
from jax.sharding import Mesh, PartitionSpec as P

ROW = ("x", "zl")
CH = ("y", "zh", "co")
CHANNELS = ("co", "x", "zl", "zh")
HOMES = ("x", "zl", "zh")
COLUMNS = ("y", "co")
PLANE = ("x", "y", "co")
DEPTH = ("zl", "zh")
F32 = jnp.float32
EPS = 1e-05


def dot(a, b, ca, cb):
    return lax.dot_general(
        a, b, (((ca,), (cb,)), ((), ())), precision=lax.Precision.HIGHEST, preferred_element_type=F32
    )


def call(body, outs, scratch=()):
    vmem = pl.BlockSpec(memory_space=pltpu.VMEM)

    def run(*args):
        return pl.pallas_call(
            body,
            out_shape=[jax.ShapeDtypeStruct(s, F32) for s in outs],
            in_specs=[vmem] * len(args),
            out_specs=[vmem] * len(outs),
            scratch_shapes=[pltpu.VMEM(s, F32) for s in scratch],
            compiler_params=pltpu.CompilerParams(vmem_limit_bytes=32 * 1024 * 1024),
        )(*args)

    return run


def norm_rows(values):
    center = values - jnp.mean(values, axis=1, keepdims=True)
    spread = jnp.mean(center * center, axis=1, keepdims=True)
    rstd = 1.0 / jnp.sqrt(spread + EPS)
    return center * rstd, rstd


def mask_lanes(mask_ref, lanes_ref):
    maskf = mask_ref[...].astype(F32)
    for ii in range(8):
        lanes_ref[0:1, ii * 16 : (ii + 1) * 16] = maskf[ii : ii + 1, :]
    return lanes_ref[0:1, :]


def enter_kernel(
    pair_hbm, mask_hbm, win_hbm, wgate_hbm, msg_ref, proj_ref, normed_ref, gate_ref,
    lanes_ref, pair_ref, mask_ref, win_ref, wgate_ref, sems
):
    sources = (pair_hbm, mask_hbm, win_hbm, wgate_hbm)
    copies = [
        pltpu.make_async_copy(source, target, sems.at[i])
        for i, (source, target) in enumerate(zip(sources, (pair_ref, mask_ref, win_ref, wgate_ref)))
    ]
    for copy in copies:
        copy.start()
    copies[0].wait()
    normed, _ = norm_rows(pair_ref[...].reshape(128, 128))
    normed_ref[...] = normed
    copies[1].wait()
    maskf = mask_lanes(mask_ref, lanes_ref)
    copies[2].wait()
    proj = dot(win_ref[...], normed, 0, 1)
    proj_ref[...] = proj
    msg_ref[:, 0, 0:128] = maskf * jax.nn.sigmoid(proj[0:128]) * proj[128:256]
    msg_ref[:, 0, 128:256] = maskf * jax.nn.sigmoid(proj[256:384]) * proj[384:512]
    copies[3].wait()
    gate_ref[...] = jax.nn.sigmoid(dot(normed, wgate_ref[...], 1, 0))


def column_blocks():
    return [
        (y * 64 + co * 32 + zh * 16, y * 64 + zh * 32 + co * 16) for y in range(4) for co in range(2) for zh in range(2)
    ]


def triangle_kernel(msg_ref, part_ref, left_ref, right_ref, flat_ref, turn_ref, natural_ref):
    flat_ref[0] = msg_ref[:, 0, 0:128]
    flat_ref[1] = msg_ref[:, 0, 128:256]
    for co in range(2):
        for zh in range(2):
            source, lanes = pl.ds(co * 64 + zh, 32, stride=2), slice(zh * 32 + co * 16, zh * 32 + co * 16 + 16)
            left, right = flat_ref[0, source, :], flat_ref[1, source, :]
            for s in range(8):
                rows = slice(s * 32, (s + 1) * 32)
                left_ref[rows, lanes] = left[:, s * 16 : (s + 1) * 16]
                turn_ref[rows, lanes] = right[:, s * 16 : (s + 1) * 16]
    for s in range(8):
        natural_ref[pl.ds(s, 32, stride=8), :] = turn_ref[s * 32 : (s + 1) * 32, :]
    for to, at in column_blocks():
        right_ref[to : to + 16, :] = natural_ref[at : at + 16, :]
    part_ref[...] = dot(right_ref[...], left_ref[...], 1, 1).reshape(8, 32, 256)


def home_kernel(part_ref, msg_ref, flat_ref, turn_ref):
    for h in range(2):
        total = ((part_ref[h] + part_ref[h + 2]) + (part_ref[h + 4] + part_ref[h + 6])).T
        for zh in range(2):
            for s in range(8):
                turn_ref[h, zh, :, s * 16 : (s + 1) * 16] = total[s * 32 : (s + 1) * 32, zh * 16 : (zh + 1) * 16]
            flat_ref[h, pl.ds(zh, 32, stride=2), :] = turn_ref[h, zh]
        msg_ref[:, 0, h * 128 : (h + 1) * 128] = flat_ref[h]


def gather_channels(msg_ref):
    return jnp.concatenate([msg_ref[:, 0, 0:128], msg_ref[:, 0, 128:256]], axis=0)


def norm_channels(values):
    center = values - jnp.mean(values, axis=0, keepdims=True)
    spread = jnp.mean(center * center, axis=0, keepdims=True)
    rstd = 1.0 / jnp.sqrt(spread + EPS)
    return center * rstd, rstd


def turn_kernel(tri_ref, cot_ref, gate_ref, wout_ref, msg_ref):
    normed, rstd = norm_channels(gather_channels(tri_ref))
    d_out = cot_ref[...].reshape(128, 128) * gate_ref[...]
    d_normed = dot(wout_ref[...], d_out, 1, 1)
    along = jnp.mean(d_normed * normed, axis=0, keepdims=True)
    d_tri = rstd * (d_normed - jnp.mean(d_normed, axis=0, keepdims=True) - normed * along)
    for h in range(2):
        msg_ref[:, 0, h * 128 : (h + 1) * 128] = d_tri[h * 64 : (h + 1) * 64]


def spread_kernel(msg_ref, out_ref, flat_ref, whole_ref):
    for h in range(2):
        flat_ref[h] = msg_ref[:, 0, h * 128 : (h + 1) * 128]
        for zh in range(2):
            block = flat_ref[h, pl.ds(zh, 32, stride=2), :]
            for s in range(8):
                whole_ref[h, s * 32 : (s + 1) * 32, zh * 16 : (zh + 1) * 16] = block[:, s * 16 : (s + 1) * 16]
        turned = whole_ref[h].T
        for y in range(4):
            out_ref[y * 2 + h] = turned


def back_kernel(dtri_ref, left_ref, right_ref, msg_ref, flat_ref, blocks_ref, natural_ref, turn_ref):
    dtri = dtri_ref[...].reshape(256, 256)
    blocks_ref[...] = dot(dtri, left_ref[...], 1, 0)
    d_left = dot(dtri, right_ref[...], 0, 0)
    for at, to in column_blocks():
        natural_ref[to : to + 16, :] = blocks_ref[at : at + 16, :]
    for s in range(8):
        d_right = natural_ref[pl.ds(s, 32, stride=8), :]
        for co in range(2):
            for zh in range(2):
                lanes = slice(zh * 32 + co * 16, zh * 32 + co * 16 + 16)
                turn_ref[0, co, zh, :, s * 16 : (s + 1) * 16] = d_left[s * 32 : (s + 1) * 32, lanes]
                turn_ref[1, co, zh, :, s * 16 : (s + 1) * 16] = d_right[:, lanes]
    for side in range(2):
        for co in range(2):
            for zh in range(2):
                flat_ref[side, pl.ds(co * 64 + zh, 32, stride=2), :] = turn_ref[side, co, zh]
        msg_ref[:, 0, side * 128 : (side + 1) * 128] = flat_ref[side]


def weights_kernel(
    msg_ref, proj_ref, normed_ref, mask_ref, tri_ref, cot_ref, gate_ref, wout_ref,
    weights_ref, dproj_ref, dpre_ref, out_ref, lanes_ref
):
    maskf = mask_lanes(mask_ref, lanes_ref)
    normed = normed_ref[...]
    normed_tri, _ = norm_channels(gather_channels(tri_ref))
    gate = gate_ref[...]
    cot = cot_ref[...].reshape(128, 128)
    out_proj = dot(normed_tri, wout_ref[...], 0, 0)
    out_ref[...] = out_proj
    d_pre = cot * out_proj * gate * (1.0 - gate)
    dpre_ref[...] = d_pre
    weights_ref[512:640] = dot(normed, d_pre, 0, 0)
    weights_ref[640:768] = dot(normed_tri, cot * gate, 1, 0)
    for side in range(2):
        base = side * 256
        d_side = maskf * msg_ref[:, 0, side * 128 : (side + 1) * 128]
        sig = jax.nn.sigmoid(proj_ref[base : base + 128])
        d_value = d_side * sig
        d_gate = d_value * proj_ref[base + 128 : base + 256] * (1.0 - sig)
        dproj_ref[base : base + 128] = d_gate
        dproj_ref[base + 128 : base + 256] = d_value
        weights_ref[base : base + 128] = dot(normed, d_gate, 0, 1)
        weights_ref[base + 128 : base + 256] = dot(normed, d_value, 0, 1)


def leave_kernel(dproj_ref, dpre_ref, out_ref, gate_ref, pair_ref, win_ref, wgate_ref, dpair_ref, upd_ref):
    upd_ref[...] = (gate_ref[...] * out_ref[...]).reshape(8, 16, 128)
    normed, rstd = norm_rows(pair_ref[...].reshape(128, 128))
    d_normed = dot(dproj_ref[...], win_ref[...], 0, 1) + dot(dpre_ref[...], wgate_ref[...], 1, 1)
    along = jnp.mean(d_normed * normed, axis=1, keepdims=True)
    d_pair = rstd * (d_normed - jnp.mean(d_normed, axis=1, keepdims=True) - normed * along)
    dpair_ref[...] = d_pair.reshape(8, 16, 128)


def sum_kernel(scale, parts_ref, out_ref):
    total = jnp.sum(parts_ref[...], axis=0) * scale
    for i in range(out_ref.shape[0]):
        out_ref[i] = total


def unpack_kernel(parts_ref, dwin_ref, dwg_ref, dwo_ref):
    whole = parts_ref[...].reshape(768, 128)
    for f in range(4):
        dwin_ref[:, f * 128 : (f + 1) * 128] = whole[f * 128 : (f + 1) * 128]
    dwg_ref[...] = whole[512:640]
    dwo_ref[...] = whole[640:768]


def swap(values, axes):
    return lax.all_to_all(values, axes, split_axis=0, concat_axis=0, tiled=True)


def enter(pair, pair_mask, w_in, w_gate):
    vmem = pl.BlockSpec(memory_space=pltpu.VMEM)
    outs = [(128, 1, 256), (512, 128), (128, 128), (128, 128)]
    return pl.pallas_call(
        enter_kernel,
        out_shape=[jax.ShapeDtypeStruct(s, F32) for s in outs],
        in_specs=[pl.BlockSpec(memory_space=pl.ANY)] * 4,
        out_specs=[vmem] * 4,
        scratch_shapes=[
            pltpu.VMEM((8, 128), F32),
            pltpu.VMEM(pair.shape, F32),
            pltpu.VMEM(pair_mask.shape, pair_mask.dtype),
            pltpu.VMEM(w_in.shape, F32),
            pltpu.VMEM(w_gate.shape, F32),
            pltpu.SemaphoreType.DMA((4,)),
        ],
        compiler_params=pltpu.CompilerParams(vmem_limit_bytes=60 * 1024 * 1024),
    )(pair, pair_mask, w_in, w_gate)


def shards(pair, pair_mask, w_in, w_gate, w_out, cotangent):
    msg, proj, normed, gate = enter(pair, pair_mask, w_in, w_gate)
    msg = swap(msg, CHANNELS)
    part, left, right = call(
        triangle_kernel, [(8, 32, 256), (256, 64), (256, 64)], [(2, 128, 128), (256, 64), (256, 64)]
    )(msg)
    part = swap(part, COLUMNS)
    (msg,) = call(home_kernel, [(64, 1, 256)], [(2, 64, 128), (2, 2, 32, 128)])(part)
    tri = swap(msg, HOMES)
    (msg,) = call(turn_kernel, [(64, 1, 256)])(tri, cotangent, gate, w_out)
    msg = swap(msg, HOMES)
    (d_tri,) = call(spread_kernel, [(8, 32, 256)], [(2, 64, 128), (2, 256, 32)])(msg)
    d_tri = swap(d_tri, COLUMNS)
    (msg,) = call(
        back_kernel, [(128, 1, 256)], [(2, 128, 128), (256, 64), (256, 64), (2, 2, 2, 32, 128)]
    )(d_tri, left, right)
    msg = swap(msg, CHANNELS)
    weights, d_proj, d_pre, out_proj = call(
        weights_kernel, [(768, 128), (512, 128), (128, 128), (128, 128)], [(8, 128)]
    )(msg, proj, normed, pair_mask, tri, cotangent, gate, w_out)
    parts = swap(weights.reshape(32, 24, 128), PLANE)
    d_pair, update = call(leave_kernel, [(8, 16, 128), (8, 16, 128)])(
        d_proj, d_pre, out_proj, gate, pair, w_in, w_gate
    )
    (parts,) = call(lambda a, b: sum_kernel(1.0, a, b), [(16, 24, 128)])(parts)
    parts = swap(parts, DEPTH)
    scale = 1.0 / (pair.shape[0] * lax.axis_size(ROW))
    (parts,) = call(lambda a, b: sum_kernel(scale, a, b), [(32, 24, 128)])(parts)
    parts = swap(parts, PLANE)
    d_win, d_wgate, d_wout = call(unpack_kernel, [(128, 512), (128, 128), (128, 128)])(parts)
    return (update, d_pair, d_win, d_wgate, d_wout)


def solution(mesh):
    fine = Mesh(mesh.devices.reshape(4, 8, 4, 2, 2), ("x", "zl", "y", "zh", "co"))
    in_specs = (P(ROW, CH, None), P(ROW, CH), P(), P(), P(), P(ROW, CH, None))
    out_specs = (P(ROW, CH, None), P(ROW, CH, None), P(), P(), P())
    return jax.shard_map(shards, mesh=fine, in_specs=in_specs, out_specs=out_specs, check_vma=False)
```

```python
import jax
import jax.numpy as jnp
from jax import lax
from jax.experimental import pallas as pl
from jax.experimental.pallas import tpu as pltpu
from jax.sharding import Mesh, PartitionSpec as P

ROW = ("x", "zl")
CH = ("y", "zh", "co")
CHANNELS = ("co", "x", "zl", "zh")
PLANE = ("x", "y", "co")
DEPTH = ("zl", "zh")
F32 = jnp.float32
EPS = 1e-05


def dot(a, b, ca, cb):
    return lax.dot_general(
        a, b, (((ca,), (cb,)), ((), ())), precision=lax.Precision.HIGHEST, preferred_element_type=F32
    )


def call(body, outs, scratch=()):
    vmem = pl.BlockSpec(memory_space=pltpu.VMEM)

    def run(*args):
        return pl.pallas_call(
            body,
            out_shape=[jax.ShapeDtypeStruct(s, F32) for s in outs],
            in_specs=[vmem] * len(args),
            out_specs=[vmem] * len(outs),
            scratch_shapes=[pltpu.VMEM(s, F32) for s in scratch],
            compiler_params=pltpu.CompilerParams(vmem_limit_bytes=32 * 1024 * 1024),
        )(*args)

    return run


def norm_rows(values):
    center = values - jnp.mean(values, axis=1, keepdims=True)
    spread = jnp.mean(center * center, axis=1, keepdims=True)
    rstd = 1.0 / jnp.sqrt(spread + EPS)
    return center * rstd, rstd


def mask_lanes(mask_ref, lanes_ref):
    maskf = mask_ref[...].astype(F32)
    for ii in range(8):
        lanes_ref[0:1, ii * 16 : (ii + 1) * 16] = maskf[ii : ii + 1, :]
    return lanes_ref[0:1, :]


def enter_kernel(
    pair_hbm, mask_hbm, win_hbm, wgate_hbm, msg_hbm, factor_hbm, normed_hbm, gate_hbm,
    pair_ref, mask_ref, win_ref, wgate_ref, msg_ref, factor_ref, normed_ref, gate_ref, lanes_ref, ins, outs
):
    pairs = ((pair_hbm, pair_ref), (mask_hbm, mask_ref), (win_hbm, win_ref), (wgate_hbm, wgate_ref))
    copies = [pltpu.make_async_copy(source, target, ins.at[i]) for i, (source, target) in enumerate(pairs)]
    pairs = ((msg_ref, msg_hbm), (factor_ref, factor_hbm), (normed_ref, normed_hbm), (gate_ref, gate_hbm))
    results = [pltpu.make_async_copy(source, target, outs.at[i]) for i, (source, target) in enumerate(pairs)]
    for copy in copies:
        copy.start()
    copies[0].wait()
    normed, _ = norm_rows(pair_ref[...].reshape(128, 128))
    normed_ref[...] = normed
    results[2].start()
    copies[1].wait()
    maskf = mask_lanes(mask_ref, lanes_ref)
    copies[2].wait()
    proj = dot(win_ref[...], normed, 0, 1)
    for side in range(2):
        base = side * 256
        value = proj[base + 128 : base + 256]
        sig = jax.nn.sigmoid(proj[base : base + 128])
        masked = maskf * sig
        msg_ref[:, 0, side * 128 : (side + 1) * 128] = masked * value
        factor_ref[base : base + 128] = masked
        factor_ref[base + 128 : base + 256] = value * (1.0 - sig)
    results[0].start()
    results[1].start()
    copies[3].wait()
    gate_ref[...] = jax.nn.sigmoid(dot(normed, wgate_ref[...], 1, 0))
    results[3].start()
    for result in results:
        result.wait()


def column_blocks():
    return [
        (y * 64 + co * 32 + zh * 16, y * 64 + zh * 32 + co * 16) for y in range(4) for co in range(2) for zh in range(2)
    ]


def triangle_kernel(msg_ref, part_ref, left_ref, right_ref, flat_ref, turn_ref, natural_ref):
    flat_ref[0] = msg_ref[:, 0, 0:128]
    flat_ref[1] = msg_ref[:, 0, 128:256]
    for co in range(2):
        for zh in range(2):
            source, lanes = pl.ds(co * 64 + zh, 32, stride=2), slice(zh * 32 + co * 16, zh * 32 + co * 16 + 16)
            left, right = flat_ref[0, source, :], flat_ref[1, source, :]
            for s in range(8):
                for x in range(4):
                    rows = slice(x * 64 + s * 8, x * 64 + s * 8 + 8)
                    left_ref[rows, lanes] = left[x * 8 : (x + 1) * 8, s * 16 : (s + 1) * 16]
                turn_ref[s * 32 : (s + 1) * 32, lanes] = right[:, s * 16 : (s + 1) * 16]
    for s in range(8):
        natural_ref[pl.ds(s, 32, stride=8), :] = turn_ref[s * 32 : (s + 1) * 32, :]
    for to, at in column_blocks():
        right_ref[to : to + 16, :] = natural_ref[at : at + 16, :]
    part = dot(right_ref[...], left_ref[...], 1, 1)
    for x, y, co, zh in plane_blocks():
        row = y * 64 + co * 32 + zh * 16
        part_ref[(x * 4 + y) * 2 + co, :, zh * 64 : (zh + 1) * 64] = part[row : row + 16, x * 64 : (x + 1) * 64]


def plane_blocks():
    return [(x, y, co, zh) for x in range(4) for y in range(4) for co in range(2) for zh in range(2)]


def home_kernel(part_ref, msg_ref, rows_ref):
    for co in range(2):
        for x in range(4):
            at, to = x * 8 + co, (co * 4 + x) * 16
            rows_ref[to : to + 16, :] = (part_ref[at] + part_ref[at + 2]) + (part_ref[at + 4] + part_ref[at + 6])
    rows_ref[...] = rows_ref[...].T
    for zl in range(8):
        for zh in range(2):
            msg_ref[zl * 2 + zh] = rows_ref[pl.ds(zh * 64 + zl, 8, stride=8), :]


def norm_channels(values):
    center = values - jnp.mean(values, axis=0, keepdims=True)
    spread = jnp.mean(center * center, axis=0, keepdims=True)
    rstd = 1.0 / jnp.sqrt(spread + EPS)
    return center * rstd, rstd


def turn_kernel(home_ref, cot_ref, gate_ref, wout_ref, msg_ref, tri_ref, flat_ref, turn_ref):
    flat_ref[...] = home_ref[...].reshape(128, 128)
    for s in range(8):
        block = flat_ref[pl.ds(s, 16, stride=8), :]
        for a in range(8):
            tri_ref[a * 16 : (a + 1) * 16, s * 16 : (s + 1) * 16] = block[:, a * 16 : (a + 1) * 16]
    normed, rstd = norm_channels(tri_ref[...])
    d_out = cot_ref[...].reshape(128, 128) * gate_ref[...]
    d_normed = dot(wout_ref[...], d_out, 1, 1)
    along = jnp.mean(d_normed * normed, axis=0, keepdims=True)
    d_tri = rstd * (d_normed - jnp.mean(d_normed, axis=0, keepdims=True) - normed * along)
    for s in range(8):
        for a in range(8):
            turn_ref[s, :, a * 16 : (a + 1) * 16] = d_tri[a * 16 : (a + 1) * 16, s * 16 : (s + 1) * 16]
        flat_ref[pl.ds(s, 16, stride=8), :] = turn_ref[s]
    msg_ref[...] = flat_ref[...].reshape(16, 8, 128)


def spread_kernel(msg_ref, out_ref, flat_ref, rows_ref):
    flat_ref[...] = msg_ref[...].reshape(128, 128)
    for zh in range(2):
        for s in range(8):
            to = zh * 64 + s * 8
            rows_ref[to : to + 8, :] = flat_ref[pl.ds(zh * 8 + s, 8, stride=16), :]
    turned = rows_ref[...].T
    for x in range(4):
        for co in range(2):
            block = turned[(co * 4 + x) * 16 : (co * 4 + x) * 16 + 16]
            for y in range(4):
                out_ref[(x * 4 + y) * 2 + co] = block


def back_kernel(
    dtri_ref, left_ref, right_ref, msg_ref, whole_ref, flat_ref, blocks_ref, natural_ref, turn_ref
):
    for x, y, co, zh in plane_blocks():
        row = y * 64 + co * 32 + zh * 16
        whole_ref[row : row + 16, x * 64 : (x + 1) * 64] = dtri_ref[
            (x * 4 + y) * 2 + co, :, zh * 64 : (zh + 1) * 64
        ]
    dtri = whole_ref[...]
    blocks_ref[...] = dot(dtri, left_ref[...], 1, 0)
    d_left = dot(dtri, right_ref[...], 0, 0)
    for at, to in column_blocks():
        natural_ref[to : to + 16, :] = blocks_ref[at : at + 16, :]
    for s in range(8):
        d_right = natural_ref[pl.ds(s, 32, stride=8), :]
        to = slice(s * 16, (s + 1) * 16)
        for co in range(2):
            for zh in range(2):
                lanes = slice(zh * 32 + co * 16, zh * 32 + co * 16 + 16)
                for x in range(4):
                    row = x * 64 + s * 8
                    turn_ref[0, co, zh, x * 8 : (x + 1) * 8, to] = d_left[row : row + 8, lanes]
                turn_ref[1, co, zh, :, to] = d_right[:, lanes]
    for side in range(2):
        for co in range(2):
            for zh in range(2):
                flat_ref[side, pl.ds(co * 64 + zh, 32, stride=2), :] = turn_ref[side, co, zh]
        msg_ref[:, 0, side * 128 : (side + 1) * 128] = flat_ref[side]


def weights_kernel(
    msg_ref, factor_ref, normed_ref, tri_ref, cot_ref, gate_ref, wout_ref, weights_ref, dproj_ref, dpre_ref, out_ref
):
    normed = normed_ref[...]
    normed_tri, _ = norm_channels(tri_ref[...])
    gate = gate_ref[...]
    cot = cot_ref[...].reshape(128, 128)
    out_proj = dot(normed_tri, wout_ref[...], 0, 0)
    out_ref[...] = out_proj
    d_pre = cot * out_proj * gate * (1.0 - gate)
    dpre_ref[...] = d_pre
    weights_ref[512:640] = dot(normed, d_pre, 0, 0)
    weights_ref[640:768] = dot(normed_tri, cot * gate, 1, 0)
    for side in range(2):
        base = side * 256
        d_value = msg_ref[:, 0, side * 128 : (side + 1) * 128] * factor_ref[base : base + 128]
        d_gate = d_value * factor_ref[base + 128 : base + 256]
        dproj_ref[base : base + 128] = d_gate
        dproj_ref[base + 128 : base + 256] = d_value
        weights_ref[base : base + 128] = dot(normed, d_gate, 0, 1)
        weights_ref[base + 128 : base + 256] = dot(normed, d_value, 0, 1)


def leave_kernel(dproj_ref, dpre_ref, out_ref, gate_ref, pair_ref, win_ref, wgate_ref, dpair_ref, upd_ref):
    upd_ref[...] = (gate_ref[...] * out_ref[...]).reshape(8, 16, 128)
    normed, rstd = norm_rows(pair_ref[...].reshape(128, 128))
    d_normed = dot(dproj_ref[...], win_ref[...], 0, 1) + dot(dpre_ref[...], wgate_ref[...], 1, 1)
    along = jnp.mean(d_normed * normed, axis=1, keepdims=True)
    d_pair = rstd * (d_normed - jnp.mean(d_normed, axis=1, keepdims=True) - normed * along)
    dpair_ref[...] = d_pair.reshape(8, 16, 128)


def sum_kernel(scale, parts_ref, out_ref):
    total = jnp.sum(parts_ref[...], axis=0) * scale
    for i in range(out_ref.shape[0]):
        out_ref[i] = total


def unpack_kernel(parts_ref, dwin_ref, dwg_ref, dwo_ref):
    whole = parts_ref[...].reshape(768, 128)
    for f in range(4):
        dwin_ref[:, f * 128 : (f + 1) * 128] = whole[f * 128 : (f + 1) * 128]
    dwg_ref[...] = whole[512:640]
    dwo_ref[...] = whole[640:768]


def swap(values, axes):
    return lax.all_to_all(values, axes, split_axis=0, concat_axis=0, tiled=True)


def enter(pair, pair_mask, w_in, w_gate):
    held = [(128, 1, 256), (512, 128), (128, 128), (128, 128)]
    return pl.pallas_call(
        enter_kernel,
        out_shape=[jax.ShapeDtypeStruct(s, F32) for s in held],
        in_specs=[pl.BlockSpec(memory_space=pl.ANY)] * 4,
        out_specs=[pl.BlockSpec(memory_space=pl.ANY)] * 4,
        scratch_shapes=[
            pltpu.VMEM(pair.shape, F32),
            pltpu.VMEM(pair_mask.shape, pair_mask.dtype),
            pltpu.VMEM(w_in.shape, F32),
            pltpu.VMEM(w_gate.shape, F32),
            *[pltpu.VMEM(s, F32) for s in held],
            pltpu.VMEM((8, 128), F32),
            pltpu.SemaphoreType.DMA((4,)),
            pltpu.SemaphoreType.DMA((4,)),
        ],
        compiler_params=pltpu.CompilerParams(vmem_limit_bytes=60 * 1024 * 1024),
    )(pair, pair_mask, w_in, w_gate)


def shards(pair, pair_mask, w_in, w_gate, w_out, cotangent):
    msg, factor, normed, gate = enter(pair, pair_mask, w_in, w_gate)
    msg = swap(msg, CHANNELS)
    part, left, right = call(
        triangle_kernel,
        [(32, 16, 128), (256, 64), (256, 64)],
        [(2, 128, 128), (256, 64), (256, 64)],
    )(msg)
    part = swap(part, PLANE)
    (msg,) = call(home_kernel, [(16, 8, 128)], [(128, 128)])(part)
    msg = swap(msg, DEPTH)
    msg, tri = call(turn_kernel, [(16, 8, 128), (128, 128)], [(128, 128), (8, 16, 128)])(
        msg, cotangent, gate, w_out
    )
    msg = swap(msg, DEPTH)
    (d_tri,) = call(spread_kernel, [(32, 16, 128)], [(128, 128), (128, 128)])(msg)
    d_tri = swap(d_tri, PLANE)
    (msg,) = call(
        back_kernel,
        [(128, 1, 256)],
        [(256, 256), (2, 128, 128), (256, 64), (256, 64), (2, 2, 2, 32, 128)],
    )(d_tri, left, right)
    msg = swap(msg, CHANNELS)
    weights, d_proj, d_pre, out_proj = call(
        weights_kernel, [(768, 128), (512, 128), (128, 128), (128, 128)]
    )(msg, factor, normed, tri, cotangent, gate, w_out)
    parts = swap(weights.reshape(32, 24, 128), PLANE)
    d_pair, update = call(leave_kernel, [(8, 16, 128), (8, 16, 128)])(
        d_proj, d_pre, out_proj, gate, pair, w_in, w_gate
    )
    (parts,) = call(lambda a, b: sum_kernel(1.0, a, b), [(16, 24, 128)])(parts)
    parts = swap(parts, DEPTH)
    scale = 1.0 / (pair.shape[0] * lax.axis_size(ROW))
    (parts,) = call(lambda a, b: sum_kernel(scale, a, b), [(32, 24, 128)])(parts)
    parts = swap(parts, PLANE)
    d_win, d_wgate, d_wout = call(unpack_kernel, [(128, 512), (128, 128), (128, 128)])(parts)
    return (update, d_pair, d_win, d_wgate, d_wout)


def solution(mesh):
    fine = Mesh(mesh.devices.reshape(4, 8, 4, 2, 2), ("x", "zl", "y", "zh", "co"))
    in_specs = (P(ROW, CH, None), P(ROW, CH), P(), P(), P(), P(ROW, CH, None))
    out_specs = (P(ROW, CH, None), P(ROW, CH, None), P(), P(), P())
    return jax.shard_map(shards, mesh=fine, in_specs=in_specs, out_specs=out_specs, check_vma=False)
```

```python
import jax
import jax.numpy as jnp
from jax import lax
from jax.experimental import pallas as pl
from jax.experimental.pallas import tpu as pltpu
from jax.sharding import Mesh, PartitionSpec as P

ROW = ("x", "zl")
CH = ("y", "zh", "co")
CHANNELS = ("co", "x", "zl", "zh")
PLANE = ("x", "y", "co")
DEPTH = ("zl", "zh")
F32 = jnp.float32
EPS = 1e-05


def dot(a, b, ca, cb):
    return lax.dot_general(
        a, b, (((ca,), (cb,)), ((), ())), precision=lax.Precision.HIGHEST, preferred_element_type=F32
    )


def call(body, outs, scratch=()):
    vmem = pl.BlockSpec(memory_space=pltpu.VMEM)

    def run(*args):
        return pl.pallas_call(
            body,
            out_shape=[jax.ShapeDtypeStruct(s, F32) for s in outs],
            in_specs=[vmem] * len(args),
            out_specs=[vmem] * len(outs),
            scratch_shapes=[pltpu.VMEM(s, F32) for s in scratch],
            compiler_params=pltpu.CompilerParams(vmem_limit_bytes=32 * 1024 * 1024),
        )(*args)

    return run


def norm_rows(values):
    center = values - jnp.mean(values, axis=1, keepdims=True)
    spread = jnp.mean(center * center, axis=1, keepdims=True)
    rstd = 1.0 / jnp.sqrt(spread + EPS)
    return center * rstd, rstd


def mask_lanes(mask_ref, lanes_ref):
    maskf = mask_ref[...].astype(F32)
    for ii in range(8):
        lanes_ref[0:1, ii * 16 : (ii + 1) * 16] = maskf[ii : ii + 1, :]
    return lanes_ref[0:1, :]


def enter_kernel(
    pair_hbm, mask_hbm, win_hbm, wgate_hbm, msg_hbm, factor_hbm, normed_hbm, gate_hbm,
    pair_ref, mask_ref, win_ref, wgate_ref, msg_ref, factor_ref, normed_ref, gate_ref, lanes_ref, ins, outs
):
    pairs = ((pair_hbm, pair_ref), (mask_hbm, mask_ref), (win_hbm, win_ref), (wgate_hbm, wgate_ref))
    copies = [pltpu.make_async_copy(source, target, ins.at[i]) for i, (source, target) in enumerate(pairs)]
    pairs = ((msg_ref, msg_hbm), (factor_ref, factor_hbm), (normed_ref, normed_hbm), (gate_ref, gate_hbm))
    results = [pltpu.make_async_copy(source, target, outs.at[i]) for i, (source, target) in enumerate(pairs)]
    for copy in copies:
        copy.start()
    copies[0].wait()
    normed, _ = norm_rows(pair_ref[...].reshape(128, 128))
    normed_ref[...] = normed
    results[2].start()
    copies[1].wait()
    maskf = mask_lanes(mask_ref, lanes_ref)
    copies[2].wait()
    proj = dot(win_ref[...], normed, 0, 1)
    for side in range(2):
        base = side * 256
        value = proj[base + 128 : base + 256]
        sig = jax.nn.sigmoid(proj[base : base + 128])
        masked = maskf * sig
        msg_ref[:, 0, side * 128 : (side + 1) * 128] = masked * value
        factor_ref[base : base + 128] = masked
        factor_ref[base + 128 : base + 256] = value * (1.0 - sig)
    results[0].start()
    results[1].start()
    copies[3].wait()
    gate_ref[...] = jax.nn.sigmoid(dot(normed, wgate_ref[...], 1, 0))
    results[3].start()
    for result in results:
        result.wait()


def column_blocks():
    return [
        (y * 64 + co * 32 + zh * 16, y * 64 + zh * 32 + co * 16) for y in range(4) for co in range(2) for zh in range(2)
    ]


def triangle_kernel(msg_ref, part_ref, left_ref, right_ref, flat_ref, turn_ref, natural_ref):
    flat_ref[0] = msg_ref[:, 0, 0:128]
    flat_ref[1] = msg_ref[:, 0, 128:256]
    for co in range(2):
        for zh in range(2):
            source, lanes = pl.ds(co * 64 + zh, 32, stride=2), slice(zh * 32 + co * 16, zh * 32 + co * 16 + 16)
            left, right = flat_ref[0, source, :], flat_ref[1, source, :]
            for s in range(8):
                for x in range(4):
                    rows = slice(x * 64 + s * 8, x * 64 + s * 8 + 8)
                    left_ref[rows, lanes] = left[x * 8 : (x + 1) * 8, s * 16 : (s + 1) * 16]
                turn_ref[s * 32 : (s + 1) * 32, lanes] = right[:, s * 16 : (s + 1) * 16]
    for s in range(8):
        natural_ref[pl.ds(s, 32, stride=8), :] = turn_ref[s * 32 : (s + 1) * 32, :]
    for to, at in column_blocks():
        right_ref[to : to + 16, :] = natural_ref[at : at + 16, :]
    part = dot(right_ref[...], left_ref[...], 1, 1)
    for x, y, co, zh in plane_blocks():
        row = y * 64 + co * 32 + zh * 16
        part_ref[(x * 4 + y) * 2 + co, :, zh * 64 : (zh + 1) * 64] = part[row : row + 16, x * 64 : (x + 1) * 64]


def plane_blocks():
    return [(x, y, co, zh) for x in range(4) for y in range(4) for co in range(2) for zh in range(2)]


def home_kernel(part_ref, msg_ref, rows_ref):
    for co in range(2):
        for x in range(4):
            at, to = x * 8 + co, (co * 4 + x) * 16
            rows_ref[to : to + 16, :] = (part_ref[at] + part_ref[at + 2]) + (part_ref[at + 4] + part_ref[at + 6])
    rows_ref[...] = rows_ref[...].T
    for zl in range(8):
        for zh in range(2):
            msg_ref[zl * 2 + zh] = rows_ref[pl.ds(zh * 64 + zl, 8, stride=8), :]


def norm_channels(values):
    center = values - jnp.mean(values, axis=0, keepdims=True)
    spread = jnp.mean(center * center, axis=0, keepdims=True)
    rstd = 1.0 / jnp.sqrt(spread + EPS)
    return center * rstd, rstd


def turn_kernel(home_ref, cot_ref, gate_ref, wout_ref, msg_ref, tri_ref, flat_ref, turn_ref):
    flat_ref[...] = home_ref[...].reshape(128, 128)
    for s in range(8):
        block = flat_ref[pl.ds(s, 16, stride=8), :]
        for a in range(8):
            tri_ref[a * 16 : (a + 1) * 16, s * 16 : (s + 1) * 16] = block[:, a * 16 : (a + 1) * 16]
    normed, rstd = norm_channels(tri_ref[...])
    d_out = cot_ref[...].reshape(128, 128) * gate_ref[...]
    d_normed = dot(wout_ref[...], d_out, 1, 1)
    along = jnp.mean(d_normed * normed, axis=0, keepdims=True)
    d_tri = rstd * (d_normed - jnp.mean(d_normed, axis=0, keepdims=True) - normed * along)
    for s in range(8):
        for a in range(8):
            turn_ref[s, :, a * 16 : (a + 1) * 16] = d_tri[a * 16 : (a + 1) * 16, s * 16 : (s + 1) * 16]
        flat_ref[pl.ds(s, 16, stride=8), :] = turn_ref[s]
    msg_ref[...] = flat_ref[...].reshape(16, 8, 128)


def spread_kernel(msg_ref, out_ref, flat_ref, rows_ref):
    flat_ref[...] = msg_ref[...].reshape(128, 128)
    for zh in range(2):
        for s in range(8):
            to = zh * 64 + s * 8
            rows_ref[to : to + 8, :] = flat_ref[pl.ds(zh * 8 + s, 8, stride=16), :]
    turned = rows_ref[...].T
    for x in range(4):
        for co in range(2):
            block = turned[(co * 4 + x) * 16 : (co * 4 + x) * 16 + 16]
            for y in range(4):
                out_ref[(x * 4 + y) * 2 + co] = block


def back_kernel(
    dtri_ref, left_ref, right_ref, msg_ref, whole_ref, flat_ref, blocks_ref, natural_ref, turn_ref
):
    for x, y, co, zh in plane_blocks():
        row = y * 64 + co * 32 + zh * 16
        whole_ref[row : row + 16, x * 64 : (x + 1) * 64] = dtri_ref[
            (x * 4 + y) * 2 + co, :, zh * 64 : (zh + 1) * 64
        ]
    dtri = whole_ref[...]
    blocks_ref[...] = dot(dtri, left_ref[...], 1, 0)
    d_left = dot(right_ref[...], dtri, 0, 0).T
    for at, to in column_blocks():
        natural_ref[to : to + 16, :] = blocks_ref[at : at + 16, :]
    for s in range(8):
        d_right = natural_ref[pl.ds(s, 32, stride=8), :]
        to = slice(s * 16, (s + 1) * 16)
        for co in range(2):
            for zh in range(2):
                lanes = slice(zh * 32 + co * 16, zh * 32 + co * 16 + 16)
                for x in range(4):
                    row = x * 64 + s * 8
                    turn_ref[0, co, zh, x * 8 : (x + 1) * 8, to] = d_left[row : row + 8, lanes]
                turn_ref[1, co, zh, :, to] = d_right[:, lanes]
    for side in range(2):
        for co in range(2):
            for zh in range(2):
                flat_ref[side, pl.ds(co * 64 + zh, 32, stride=2), :] = turn_ref[side, co, zh]
        msg_ref[:, 0, side * 128 : (side + 1) * 128] = flat_ref[side]


def weights_kernel(
    msg_ref, factor_ref, normed_ref, tri_ref, cot_ref, gate_ref, wout_ref, weights_ref, dproj_ref, dpre_ref, out_ref
):
    normed = normed_ref[...]
    normed_tri, _ = norm_channels(tri_ref[...])
    gate = gate_ref[...]
    cot = cot_ref[...].reshape(128, 128)
    out_proj = dot(normed_tri, wout_ref[...], 0, 0)
    out_ref[...] = out_proj
    d_pre = cot * out_proj * gate * (1.0 - gate)
    dpre_ref[...] = d_pre
    weights_ref[512:640] = dot(normed, d_pre, 0, 0)
    weights_ref[640:768] = dot(normed_tri, cot * gate, 1, 0)
    for side in range(2):
        base = side * 256
        d_value = msg_ref[:, 0, side * 128 : (side + 1) * 128] * factor_ref[base : base + 128]
        d_gate = d_value * factor_ref[base + 128 : base + 256]
        dproj_ref[base : base + 128] = d_gate
        dproj_ref[base + 128 : base + 256] = d_value
    d_win = dot(normed, dproj_ref[...], 0, 1)
    for f in range(4):
        weights_ref[f * 128 : (f + 1) * 128] = d_win[:, f * 128 : (f + 1) * 128]


def sum_kernel(scale, parts_ref, out_ref):
    total = jnp.sum(parts_ref[...], axis=0) * scale
    for i in range(out_ref.shape[0]):
        out_ref[i] = total


def leave_kernel(
    parts_ref, dproj_ref, dpre_ref, out_ref, gate_ref, pair_ref, win_ref, wgate_ref,
    dpair_ref, upd_ref, dwin_ref, dwg_ref, dwo_ref
):
    for f in range(4):
        dwin_ref[:, f * 128 : (f + 1) * 128] = parts_ref[...].reshape(768, 128)[f * 128 : (f + 1) * 128]
    dwg_ref[...] = parts_ref[...].reshape(768, 128)[512:640]
    dwo_ref[...] = parts_ref[...].reshape(768, 128)[640:768]
    upd_ref[...] = (gate_ref[...] * out_ref[...]).reshape(8, 16, 128)
    normed, rstd = norm_rows(pair_ref[...].reshape(128, 128))
    d_normed = dot(dproj_ref[...], win_ref[...], 0, 1) + dot(dpre_ref[...], wgate_ref[...], 1, 1)
    along = jnp.mean(d_normed * normed, axis=1, keepdims=True)
    d_pair = rstd * (d_normed - jnp.mean(d_normed, axis=1, keepdims=True) - normed * along)
    dpair_ref[...] = d_pair.reshape(8, 16, 128)


def swap(values, axes):
    return lax.all_to_all(values, axes, split_axis=0, concat_axis=0, tiled=True)


def enter(pair, pair_mask, w_in, w_gate):
    held = [(128, 1, 256), (512, 128), (128, 128), (128, 128)]
    return pl.pallas_call(
        enter_kernel,
        out_shape=[jax.ShapeDtypeStruct(s, F32) for s in held],
        in_specs=[pl.BlockSpec(memory_space=pl.ANY)] * 4,
        out_specs=[pl.BlockSpec(memory_space=pl.ANY)] * 4,
        scratch_shapes=[
            pltpu.VMEM(pair.shape, F32),
            pltpu.VMEM(pair_mask.shape, pair_mask.dtype),
            pltpu.VMEM(w_in.shape, F32),
            pltpu.VMEM(w_gate.shape, F32),
            *[pltpu.VMEM(s, F32) for s in held],
            pltpu.VMEM((8, 128), F32),
            pltpu.SemaphoreType.DMA((4,)),
            pltpu.SemaphoreType.DMA((4,)),
        ],
        compiler_params=pltpu.CompilerParams(vmem_limit_bytes=60 * 1024 * 1024),
    )(pair, pair_mask, w_in, w_gate)


def shards(pair, pair_mask, w_in, w_gate, w_out, cotangent):
    msg, factor, normed, gate = enter(pair, pair_mask, w_in, w_gate)
    msg = swap(msg, CHANNELS)
    part, left, right = call(
        triangle_kernel,
        [(32, 16, 128), (256, 64), (256, 64)],
        [(2, 128, 128), (256, 64), (256, 64)],
    )(msg)
    part = swap(part, PLANE)
    (msg,) = call(home_kernel, [(16, 8, 128)], [(128, 128)])(part)
    msg = swap(msg, DEPTH)
    msg, tri = call(turn_kernel, [(16, 8, 128), (128, 128)], [(128, 128), (8, 16, 128)])(
        msg, cotangent, gate, w_out
    )
    msg = swap(msg, DEPTH)
    (d_tri,) = call(spread_kernel, [(32, 16, 128)], [(128, 128), (128, 128)])(msg)
    d_tri = swap(d_tri, PLANE)
    (msg,) = call(
        back_kernel,
        [(128, 1, 256)],
        [(256, 256), (2, 128, 128), (256, 64), (256, 64), (2, 2, 2, 32, 128)],
    )(d_tri, left, right)
    msg = swap(msg, CHANNELS)
    weights, d_proj, d_pre, out_proj = call(
        weights_kernel, [(768, 128), (512, 128), (128, 128), (128, 128)]
    )(msg, factor, normed, tri, cotangent, gate, w_out)
    parts = swap(weights.reshape(32, 24, 128), PLANE)
    (parts,) = call(lambda a, b: sum_kernel(1.0, a, b), [(16, 24, 128)])(parts)
    parts = swap(parts, DEPTH)
    scale = 1.0 / (pair.shape[0] * lax.axis_size(ROW))
    (parts,) = call(lambda a, b: sum_kernel(scale, a, b), [(32, 24, 128)])(parts)
    parts = swap(parts, PLANE)
    d_pair, update, d_win, d_wgate, d_wout = call(
        leave_kernel, [(8, 16, 128), (8, 16, 128), (128, 512), (128, 128), (128, 128)]
    )(parts, d_proj, d_pre, out_proj, gate, pair, w_in, w_gate)
    return (update, d_pair, d_win, d_wgate, d_wout)


def solution(mesh):
    fine = Mesh(mesh.devices.reshape(4, 8, 4, 2, 2), ("x", "zl", "y", "zh", "co"))
    in_specs = (P(ROW, CH, None), P(ROW, CH), P(), P(), P(), P(ROW, CH, None))
    out_specs = (P(ROW, CH, None), P(ROW, CH, None), P(), P(), P())
    return jax.shard_map(shards, mesh=fine, in_specs=in_specs, out_specs=out_specs, check_vma=False)
```

```python
import jax
import jax.numpy as jnp
from jax import lax
from jax.experimental import pallas as pl
from jax.experimental.pallas import tpu as pltpu
from jax.sharding import Mesh, PartitionSpec as P

ROW = ("x", "zl")
CH = ("y", "zh", "co")
CHANNELS = ("zl", "zh", "co", "x")
PLANE = ("x", "y", "co")
DEPTH = ("zl", "zh")
F32 = jnp.float32
EPS = 1e-05


def dot(a, b, ca, cb):
    return lax.dot_general(
        a, b, (((ca,), (cb,)), ((), ())), precision=lax.Precision.HIGHEST, preferred_element_type=F32
    )


def call(body, outs, scratch=()):
    vmem = pl.BlockSpec(memory_space=pltpu.VMEM)

    def run(*args):
        return pl.pallas_call(
            body,
            out_shape=[jax.ShapeDtypeStruct(s, F32) for s in outs],
            in_specs=[vmem] * len(args),
            out_specs=[vmem] * len(outs),
            scratch_shapes=[pltpu.VMEM(s, F32) for s in scratch],
            compiler_params=pltpu.CompilerParams(vmem_limit_bytes=32 * 1024 * 1024),
        )(*args)

    return run


def norm_rows(values):
    center = values - jnp.mean(values, axis=1, keepdims=True)
    spread = jnp.mean(center * center, axis=1, keepdims=True)
    rstd = 1.0 / jnp.sqrt(spread + EPS)
    return center * rstd, rstd


def mask_lanes(mask_ref, lanes_ref):
    maskf = mask_ref[...].astype(F32)
    for ii in range(8):
        lanes_ref[0:1, ii * 16 : (ii + 1) * 16] = maskf[ii : ii + 1, :]
    return lanes_ref[0:1, :]


def enter_kernel(
    pair_hbm, mask_hbm, win_hbm, wgate_hbm, msg_hbm, factor_hbm, normed_hbm, gate_hbm,
    pair_ref, mask_ref, win_ref, wgate_ref, msg_ref, factor_ref, normed_ref, gate_ref, lanes_ref, ins, outs
):
    pairs = ((pair_hbm, pair_ref), (mask_hbm, mask_ref), (win_hbm, win_ref), (wgate_hbm, wgate_ref))
    copies = [pltpu.make_async_copy(source, target, ins.at[i]) for i, (source, target) in enumerate(pairs)]
    pairs = ((msg_ref, msg_hbm), (factor_ref, factor_hbm), (normed_ref, normed_hbm), (gate_ref, gate_hbm))
    results = [pltpu.make_async_copy(source, target, outs.at[i]) for i, (source, target) in enumerate(pairs)]
    for copy in copies:
        copy.start()
    copies[0].wait()
    normed, _ = norm_rows(pair_ref[...].reshape(128, 128))
    normed_ref[...] = normed
    results[2].start()
    copies[1].wait()
    maskf = mask_lanes(mask_ref, lanes_ref)
    copies[2].wait()
    proj = dot(win_ref[...], normed, 0, 1)
    for side in range(2):
        base = side * 256
        value = proj[base + 128 : base + 256]
        sig = jax.nn.sigmoid(proj[base : base + 128])
        masked = maskf * sig
        msg_ref[:, 0, side * 128 : (side + 1) * 128] = masked * value
        factor_ref[base : base + 128] = masked
        factor_ref[base + 128 : base + 256] = value * (1.0 - sig)
    results[0].start()
    results[1].start()
    copies[3].wait()
    gate_ref[...] = jax.nn.sigmoid(dot(normed, wgate_ref[...], 1, 0))
    results[3].start()
    for result in results:
        result.wait()


def column_blocks():
    return [
        (y * 64 + co * 32 + zh * 16, y * 64 + zh * 32 + co * 16) for y in range(4) for co in range(2) for zh in range(2)
    ]


def triangle_kernel(msg_ref, part_ref, left_ref, right_ref, flat_ref, turn_ref, natural_ref):
    flat_ref[0, 0:128] = msg_ref[:, 0, 0:128]
    flat_ref[1, 0:128] = msg_ref[:, 0, 128:256]
    for x, co, zh in channel_blocks():
        source, lanes = pl.ds(zh * 8 + co * 4 + x, 8, stride=16), slice(zh * 32 + co * 16, zh * 32 + co * 16 + 16)
        left, right = flat_ref[0, source, :], flat_ref[1, source, :]
        for s in range(8):
            left_ref[x * 64 + s * 8 : x * 64 + s * 8 + 8, lanes] = left[:, s * 16 : (s + 1) * 16]
            turn_ref[s * 32 + x * 8 : s * 32 + x * 8 + 8, lanes] = right[:, s * 16 : (s + 1) * 16]
    for s in range(8):
        natural_ref[pl.ds(s, 32, stride=8), :] = turn_ref[s * 32 : (s + 1) * 32, :]
    for to, at in column_blocks():
        right_ref[to : to + 16, :] = natural_ref[at : at + 16, :]
    part = dot(right_ref[...], left_ref[...], 1, 1)
    for x, y, co, zh in plane_blocks():
        row = y * 64 + co * 32 + zh * 16
        part_ref[(x * 4 + y) * 2 + co, :, zh * 64 : (zh + 1) * 64] = part[row : row + 16, x * 64 : (x + 1) * 64]


def channel_blocks():
    return [(x, co, zh) for x in range(4) for co in range(2) for zh in range(2)]


def plane_blocks():
    return [(x, y, co, zh) for x in range(4) for y in range(4) for co in range(2) for zh in range(2)]


def home_kernel(part_ref, msg_ref, rows_ref):
    for co in range(2):
        for x in range(4):
            at, to = x * 8 + co, (co * 4 + x) * 16
            rows_ref[to : to + 16, :] = (part_ref[at] + part_ref[at + 2]) + (part_ref[at + 4] + part_ref[at + 6])
    rows_ref[0:128] = rows_ref[0:128].T
    for zl in range(8):
        for zh in range(2):
            msg_ref[zl * 2 + zh] = rows_ref[pl.ds(zh * 64 + zl, 8, stride=8), :]


def norm_channels(values):
    center = values - jnp.mean(values, axis=0, keepdims=True)
    spread = jnp.mean(center * center, axis=0, keepdims=True)
    rstd = 1.0 / jnp.sqrt(spread + EPS)
    return center * rstd, rstd


def turn_kernel(home_ref, cot_ref, gate_ref, wout_ref, msg_ref, tri_ref, flat_ref, turn_ref):
    flat_ref[0:128] = home_ref[...].reshape(128, 128)
    for s in range(8):
        block = flat_ref[pl.ds(s, 16, stride=8), :]
        for a in range(8):
            turn_ref[a, :, s * 16 : (s + 1) * 16] = block[:, a * 16 : (a + 1) * 16]
    for a in range(8):
        flat_ref[pl.ds(a, 16, stride=8), :] = turn_ref[a]
    tri = flat_ref[0:128]
    tri_ref[...] = tri
    normed, rstd = norm_channels(tri)
    d_out = cot_ref[...].reshape(128, 128) * gate_ref[...]
    d_normed = dot(wout_ref[...], d_out, 1, 1)
    along = jnp.mean(d_normed * normed, axis=0, keepdims=True)
    flat_ref[0:128] = rstd * (d_normed - jnp.mean(d_normed, axis=0, keepdims=True) - normed * along)
    for a in range(8):
        block = flat_ref[pl.ds(a, 16, stride=8), :]
        for s in range(8):
            turn_ref[s, :, a * 16 : (a + 1) * 16] = block[:, s * 16 : (s + 1) * 16]
    for s in range(8):
        flat_ref[pl.ds(s, 16, stride=8), :] = turn_ref[s]
    msg_ref[...] = flat_ref[0:128].reshape(16, 8, 128)


def spread_kernel(msg_ref, out_ref, flat_ref, rows_ref):
    flat_ref[0:128] = msg_ref[...].reshape(128, 128)
    for zh in range(2):
        for s in range(8):
            to = zh * 64 + s * 8
            rows_ref[to : to + 8, :] = flat_ref[pl.ds(zh * 8 + s, 8, stride=16), :]
    turned = rows_ref[...].T
    for x in range(4):
        for co in range(2):
            block = turned[(co * 4 + x) * 16 : (co * 4 + x) * 16 + 16]
            for y in range(4):
                out_ref[(x * 4 + y) * 2 + co] = block


def back_kernel(
    dtri_ref, left_ref, right_ref, msg_ref, whole_ref, flat_ref, blocks_ref, natural_ref, turn_ref
):
    for x, y, co, zh in plane_blocks():
        row = y * 64 + co * 32 + zh * 16
        whole_ref[row : row + 16, x * 64 : (x + 1) * 64] = dtri_ref[
            (x * 4 + y) * 2 + co, :, zh * 64 : (zh + 1) * 64
        ]
    dtri = whole_ref[...]
    blocks_ref[...] = dot(dtri, left_ref[...], 1, 0)
    d_left = dot(right_ref[...], dtri, 0, 0).T
    for at, to in column_blocks():
        natural_ref[to : to + 16, :] = blocks_ref[at : at + 16, :]
    for s in range(8):
        d_right = natural_ref[pl.ds(s, 32, stride=8), :]
        to = slice(s * 16, (s + 1) * 16)
        for x, co, zh in channel_blocks():
            lanes = slice(zh * 32 + co * 16, zh * 32 + co * 16 + 16)
            turn_ref[0, co, zh, x, :, to] = d_left[x * 64 + s * 8 : x * 64 + s * 8 + 8, lanes]
            turn_ref[1, co, zh, x, :, to] = d_right[x * 8 : (x + 1) * 8, lanes]
    for side in range(2):
        for x, co, zh in channel_blocks():
            flat_ref[side, pl.ds(zh * 8 + co * 4 + x, 8, stride=16), :] = turn_ref[side, co, zh, x]
        msg_ref[:, 0, side * 128 : (side + 1) * 128] = flat_ref[side, 0:128]


def weights_kernel(
    msg_ref, factor_ref, normed_ref, tri_ref, cot_ref, gate_ref, wout_ref, weights_ref, dproj_ref, dpre_ref, out_ref
):
    normed = normed_ref[...]
    normed_tri, _ = norm_channels(tri_ref[...])
    gate = gate_ref[...]
    cot = cot_ref[...].reshape(128, 128)
    out_proj = dot(normed_tri, wout_ref[...], 0, 0)
    out_ref[...] = out_proj
    d_pre = cot * out_proj * gate * (1.0 - gate)
    dpre_ref[...] = d_pre
    weights_ref[512:640] = dot(normed, d_pre, 0, 0)
    weights_ref[640:768] = dot(normed_tri, cot * gate, 1, 0)
    for side in range(2):
        base = side * 256
        d_value = msg_ref[:, 0, side * 128 : (side + 1) * 128] * factor_ref[base : base + 128]
        d_gate = d_value * factor_ref[base + 128 : base + 256]
        dproj_ref[base : base + 128] = d_gate
        dproj_ref[base + 128 : base + 256] = d_value
    d_win = dot(normed, dproj_ref[...], 0, 1)
    for f in range(4):
        weights_ref[f * 128 : (f + 1) * 128] = d_win[:, f * 128 : (f + 1) * 128]


def sum_kernel(scale, parts_ref, out_ref):
    total = jnp.sum(parts_ref[...], axis=0) * scale
    for i in range(out_ref.shape[0]):
        out_ref[i] = total


def leave_kernel(
    parts_ref, dproj_ref, dpre_ref, out_ref, gate_ref, pair_ref, win_ref, wgate_ref,
    dpair_ref, upd_ref, dwin_ref, dwg_ref, dwo_ref
):
    for f in range(4):
        dwin_ref[:, f * 128 : (f + 1) * 128] = parts_ref[...].reshape(768, 128)[f * 128 : (f + 1) * 128]
    dwg_ref[...] = parts_ref[...].reshape(768, 128)[512:640]
    dwo_ref[...] = parts_ref[...].reshape(768, 128)[640:768]
    upd_ref[...] = (gate_ref[...] * out_ref[...]).reshape(8, 16, 128)
    normed, rstd = norm_rows(pair_ref[...].reshape(128, 128))
    d_normed = dot(dproj_ref[...], win_ref[...], 0, 1) + dot(dpre_ref[...], wgate_ref[...], 1, 1)
    along = jnp.mean(d_normed * normed, axis=1, keepdims=True)
    d_pair = rstd * (d_normed - jnp.mean(d_normed, axis=1, keepdims=True) - normed * along)
    dpair_ref[...] = d_pair.reshape(8, 16, 128)


def swap(values, axes):
    return lax.all_to_all(values, axes, split_axis=0, concat_axis=0, tiled=True)


def enter(pair, pair_mask, w_in, w_gate):
    held = [(128, 1, 256), (512, 128), (128, 128), (128, 128)]
    return pl.pallas_call(
        enter_kernel,
        out_shape=[jax.ShapeDtypeStruct(s, F32) for s in held],
        in_specs=[pl.BlockSpec(memory_space=pl.ANY)] * 4,
        out_specs=[pl.BlockSpec(memory_space=pl.ANY)] * 4,
        scratch_shapes=[
            pltpu.VMEM(pair.shape, F32),
            pltpu.VMEM(pair_mask.shape, pair_mask.dtype),
            pltpu.VMEM(w_in.shape, F32),
            pltpu.VMEM(w_gate.shape, F32),
            *[pltpu.VMEM(s, F32) for s in held],
            pltpu.VMEM((8, 128), F32),
            pltpu.SemaphoreType.DMA((4,)),
            pltpu.SemaphoreType.DMA((4,)),
        ],
        compiler_params=pltpu.CompilerParams(vmem_limit_bytes=60 * 1024 * 1024),
    )(pair, pair_mask, w_in, w_gate)


def shards(pair, pair_mask, w_in, w_gate, w_out, cotangent):
    msg, factor, normed, gate = enter(pair, pair_mask, w_in, w_gate)
    msg = swap(msg, CHANNELS)
    part, left, right = call(
        triangle_kernel,
        [(32, 16, 128), (256, 64), (256, 64)],
        [(2, 144, 128), (256, 64), (264, 64)],
    )(msg)
    part = swap(part, PLANE)
    (msg,) = call(home_kernel, [(16, 8, 128)], [(136, 128)])(part)
    msg = swap(msg, DEPTH)
    msg, tri = call(turn_kernel, [(16, 8, 128), (128, 128)], [(136, 128), (8, 16, 128)])(
        msg, cotangent, gate, w_out
    )
    msg = swap(msg, DEPTH)
    (d_tri,) = call(spread_kernel, [(32, 16, 128)], [(144, 128), (128, 128)])(msg)
    d_tri = swap(d_tri, PLANE)
    (msg,) = call(
        back_kernel,
        [(128, 1, 256)],
        [(256, 256), (2, 144, 128), (256, 64), (264, 64), (2, 2, 2, 4, 8, 128)],
    )(d_tri, left, right)
    msg = swap(msg, CHANNELS)
    weights, d_proj, d_pre, out_proj = call(
        weights_kernel, [(768, 128), (512, 128), (128, 128), (128, 128)]
    )(msg, factor, normed, tri, cotangent, gate, w_out)
    parts = swap(weights.reshape(32, 24, 128), PLANE)
    (parts,) = call(lambda a, b: sum_kernel(1.0, a, b), [(16, 24, 128)])(parts)
    parts = swap(parts, DEPTH)
    scale = 1.0 / (pair.shape[0] * lax.axis_size(ROW))
    (parts,) = call(lambda a, b: sum_kernel(scale, a, b), [(32, 24, 128)])(parts)
    parts = swap(parts, PLANE)
    d_pair, update, d_win, d_wgate, d_wout = call(
        leave_kernel, [(8, 16, 128), (8, 16, 128), (128, 512), (128, 128), (128, 128)]
    )(parts, d_proj, d_pre, out_proj, gate, pair, w_in, w_gate)
    return (update, d_pair, d_win, d_wgate, d_wout)


def solution(mesh):
    fine = Mesh(mesh.devices.reshape(4, 8, 4, 2, 2), ("x", "zl", "y", "zh", "co"))
    in_specs = (P(ROW, CH, None), P(ROW, CH), P(), P(), P(), P(ROW, CH, None))
    out_specs = (P(ROW, CH, None), P(ROW, CH, None), P(), P(), P())
    return jax.shard_map(shards, mesh=fine, in_specs=in_specs, out_specs=out_specs, check_vma=False)
```

```python
import jax
import jax.numpy as jnp
from jax import lax
from jax.experimental import pallas as pl
from jax.experimental.pallas import tpu as pltpu
from jax.sharding import Mesh, PartitionSpec as P

ROW = ("x", "zl")
CH = ("y", "zh", "co")
CHANNELS = ("zh", "zl", "co", "x")
PLANE = ("x", "y", "co")
DEPTH = ("zh", "zl")
F32 = jnp.float32
EPS = 1e-05


def dot(a, b, ca, cb):
    return lax.dot_general(
        a, b, (((ca,), (cb,)), ((), ())), precision=lax.Precision.HIGHEST, preferred_element_type=F32
    )


def call(body, outs, scratch=()):
    vmem = pl.BlockSpec(memory_space=pltpu.VMEM)

    def run(*args):
        return pl.pallas_call(
            body,
            out_shape=[jax.ShapeDtypeStruct(s, F32) for s in outs],
            in_specs=[vmem] * len(args),
            out_specs=[vmem] * len(outs),
            scratch_shapes=[pltpu.VMEM(s, F32) for s in scratch],
            compiler_params=pltpu.CompilerParams(vmem_limit_bytes=32 * 1024 * 1024),
        )(*args)

    return run


def norm_rows(values):
    center = values - jnp.mean(values, axis=1, keepdims=True)
    spread = jnp.mean(center * center, axis=1, keepdims=True)
    rstd = 1.0 / jnp.sqrt(spread + EPS)
    return center * rstd, rstd


def mask_lanes(mask_ref, lanes_ref):
    maskf = mask_ref[...].astype(F32)
    for ii in range(8):
        lanes_ref[0:1, ii * 16 : (ii + 1) * 16] = maskf[ii : ii + 1, :]
    return lanes_ref[0:1, :]


def enter_kernel(
    pair_hbm, mask_hbm, win_hbm, wgate_hbm, msg_hbm, factor_hbm, normed_hbm, gate_hbm,
    pair_ref, mask_ref, win_ref, wgate_ref, msg_ref, factor_ref, normed_ref, gate_ref, lanes_ref, ins, outs
):
    pairs = ((pair_hbm, pair_ref), (mask_hbm, mask_ref), (win_hbm, win_ref), (wgate_hbm, wgate_ref))
    copies = [pltpu.make_async_copy(source, target, ins.at[i]) for i, (source, target) in enumerate(pairs)]
    pairs = ((msg_ref, msg_hbm), (factor_ref, factor_hbm), (normed_ref, normed_hbm), (gate_ref, gate_hbm))
    results = [pltpu.make_async_copy(source, target, outs.at[i]) for i, (source, target) in enumerate(pairs)]
    for copy in copies:
        copy.start()
    copies[0].wait()
    normed, _ = norm_rows(pair_ref[...].reshape(128, 128))
    normed_ref[...] = normed
    results[2].start()
    copies[1].wait()
    maskf = mask_lanes(mask_ref, lanes_ref)
    copies[2].wait()
    proj = dot(win_ref[...], normed, 0, 1)
    for side in range(2):
        base = side * 256
        value = proj[base + 128 : base + 256]
        sig = jax.nn.sigmoid(proj[base : base + 128])
        masked = maskf * sig
        msg_ref[:, 0, side * 128 : (side + 1) * 128] = masked * value
        factor_ref[base : base + 128] = masked
        factor_ref[base + 128 : base + 256] = value * (1.0 - sig)
    results[0].start()
    results[1].start()
    copies[3].wait()
    gate_ref[...] = jax.nn.sigmoid(dot(normed, wgate_ref[...], 1, 0))
    results[3].start()
    for result in results:
        result.wait()


def column_blocks():
    return [
        (y * 64 + co * 32 + zh * 16, y * 64 + zh * 32 + co * 16) for y in range(4) for co in range(2) for zh in range(2)
    ]


def triangle_kernel(msg_ref, part_ref, left_ref, right_ref, flat_ref, turn_ref, natural_ref):
    flat_ref[0, 0:128] = msg_ref[:, 0, 0:128]
    flat_ref[1, 0:128] = msg_ref[:, 0, 128:256]
    for x, co, zh in channel_blocks():
        source, lanes = pl.ds(zh * 64 + co * 4 + x, 8, stride=8), slice(zh * 32 + co * 16, zh * 32 + co * 16 + 16)
        left, right = flat_ref[0, source, :], flat_ref[1, source, :]
        for s in range(8):
            left_ref[x * 64 + s * 8 : x * 64 + s * 8 + 8, lanes] = left[:, s * 16 : (s + 1) * 16]
            turn_ref[s * 32 + x * 8 : s * 32 + x * 8 + 8, lanes] = right[:, s * 16 : (s + 1) * 16]
    for s in range(8):
        natural_ref[pl.ds(s, 32, stride=8), :] = turn_ref[s * 32 : (s + 1) * 32, :]
    for to, at in column_blocks():
        right_ref[to : to + 16, :] = natural_ref[at : at + 16, :]
    part = dot(right_ref[...], left_ref[...], 1, 1)
    for x, y, co, zh in plane_blocks():
        row = y * 64 + co * 32 + zh * 16
        part_ref[(x * 4 + y) * 2 + co, :, zh * 64 : (zh + 1) * 64] = part[row : row + 16, x * 64 : (x + 1) * 64]


def channel_blocks():
    return [(x, co, zh) for x in range(4) for co in range(2) for zh in range(2)]


def plane_blocks():
    return [(x, y, co, zh) for x in range(4) for y in range(4) for co in range(2) for zh in range(2)]


def home_kernel(part_ref, msg_ref, rows_ref):
    for co in range(2):
        for x in range(4):
            at, to = x * 8 + co, (co * 4 + x) * 16
            rows_ref[to : to + 16, :] = (part_ref[at] + part_ref[at + 2]) + (part_ref[at + 4] + part_ref[at + 6])
    rows_ref[0:128] = rows_ref[0:128].T
    for zl in range(8):
        for zh in range(2):
            msg_ref[zh * 8 + zl] = rows_ref[pl.ds(zh * 64 + zl, 8, stride=8), :]


def norm_channels(values):
    center = values - jnp.mean(values, axis=0, keepdims=True)
    spread = jnp.mean(center * center, axis=0, keepdims=True)
    rstd = 1.0 / jnp.sqrt(spread + EPS)
    return center * rstd, rstd


def turn_kernel(home_ref, cot_ref, gate_ref, wout_ref, msg_ref, tri_ref, flat_ref, turn_ref):
    flat_ref[0:128] = home_ref[...].reshape(128, 128)
    for s in range(8):
        block = flat_ref[pl.ds(s, 16, stride=8), :]
        for a in range(8):
            turn_ref[a, :, s * 16 : (s + 1) * 16] = block[:, a * 16 : (a + 1) * 16]
    for a in range(8):
        flat_ref[pl.ds(a, 16, stride=8), :] = turn_ref[a]
    tri = flat_ref[0:128]
    tri_ref[...] = tri
    normed, rstd = norm_channels(tri)
    d_out = cot_ref[...].reshape(128, 128) * gate_ref[...]
    d_normed = dot(wout_ref[...], d_out, 1, 1)
    along = jnp.mean(d_normed * normed, axis=0, keepdims=True)
    flat_ref[0:128] = rstd * (d_normed - jnp.mean(d_normed, axis=0, keepdims=True) - normed * along)
    for a in range(8):
        block = flat_ref[pl.ds(a, 16, stride=8), :]
        for s in range(8):
            turn_ref[s, :, a * 16 : (a + 1) * 16] = block[:, s * 16 : (s + 1) * 16]
    for s in range(8):
        flat_ref[pl.ds(s, 16, stride=8), :] = turn_ref[s]
    msg_ref[...] = flat_ref[0:128].reshape(16, 8, 128)


def spread_kernel(msg_ref, out_ref, flat_ref, rows_ref):
    flat_ref[0:128] = msg_ref[...].reshape(128, 128)
    for zh in range(2):
        for s in range(8):
            to = zh * 64 + s * 8
            rows_ref[to : to + 8, :] = flat_ref[pl.ds(zh * 64 + s, 8, stride=8), :]
    turned = rows_ref[...].T
    for x in range(4):
        for co in range(2):
            block = turned[(co * 4 + x) * 16 : (co * 4 + x) * 16 + 16]
            for y in range(4):
                out_ref[(x * 4 + y) * 2 + co] = block


def back_kernel(
    dtri_ref, left_ref, right_ref, msg_ref, whole_ref, flat_ref, blocks_ref, natural_ref, turn_ref
):
    for x, y, co, zh in plane_blocks():
        row = y * 64 + co * 32 + zh * 16
        whole_ref[row : row + 16, x * 64 : (x + 1) * 64] = dtri_ref[
            (x * 4 + y) * 2 + co, :, zh * 64 : (zh + 1) * 64
        ]
    dtri = whole_ref[...]
    blocks_ref[...] = dot(dtri, left_ref[...], 1, 0)
    d_left = dot(right_ref[...], dtri, 0, 0).T
    for at, to in column_blocks():
        natural_ref[to : to + 16, :] = blocks_ref[at : at + 16, :]
    for s in range(8):
        d_right = natural_ref[pl.ds(s, 32, stride=8), :]
        to = slice(s * 16, (s + 1) * 16)
        for x, co, zh in channel_blocks():
            lanes = slice(zh * 32 + co * 16, zh * 32 + co * 16 + 16)
            turn_ref[0, co, zh, x, :, to] = d_left[x * 64 + s * 8 : x * 64 + s * 8 + 8, lanes]
            turn_ref[1, co, zh, x, :, to] = d_right[x * 8 : (x + 1) * 8, lanes]
    for side in range(2):
        for x, co, zh in channel_blocks():
            flat_ref[side, pl.ds(zh * 64 + co * 4 + x, 8, stride=8), :] = turn_ref[side, co, zh, x]
        msg_ref[:, 0, side * 128 : (side + 1) * 128] = flat_ref[side, 0:128]


def weights_kernel(
    msg_ref, factor_ref, normed_ref, tri_ref, cot_ref, gate_ref, wout_ref, weights_ref, dproj_ref, dpre_ref, out_ref
):
    normed = normed_ref[...]
    normed_tri, _ = norm_channels(tri_ref[...])
    gate = gate_ref[...]
    cot = cot_ref[...].reshape(128, 128)
    out_proj = dot(normed_tri, wout_ref[...], 0, 0)
    out_ref[...] = out_proj
    d_pre = cot * out_proj * gate * (1.0 - gate)
    dpre_ref[...] = d_pre
    weights_ref[512:640] = dot(normed, d_pre, 0, 0)
    weights_ref[640:768] = dot(normed_tri, cot * gate, 1, 0)
    for side in range(2):
        base = side * 256
        d_value = msg_ref[:, 0, side * 128 : (side + 1) * 128] * factor_ref[base : base + 128]
        d_gate = d_value * factor_ref[base + 128 : base + 256]
        dproj_ref[base : base + 128] = d_gate
        dproj_ref[base + 128 : base + 256] = d_value
    d_win = dot(normed, dproj_ref[...], 0, 1)
    for f in range(4):
        weights_ref[f * 128 : (f + 1) * 128] = d_win[:, f * 128 : (f + 1) * 128]


def sum_kernel(scale, parts_ref, out_ref):
    total = jnp.sum(parts_ref[...], axis=0) * scale
    for i in range(out_ref.shape[0]):
        out_ref[i] = total


def leave_kernel(
    parts_ref, dproj_ref, dpre_ref, out_ref, gate_ref, pair_ref, win_ref, wgate_ref,
    dpair_ref, upd_ref, dwin_ref, dwg_ref, dwo_ref
):
    for f in range(4):
        dwin_ref[:, f * 128 : (f + 1) * 128] = parts_ref[...].reshape(768, 128)[f * 128 : (f + 1) * 128]
    dwg_ref[...] = parts_ref[...].reshape(768, 128)[512:640]
    dwo_ref[...] = parts_ref[...].reshape(768, 128)[640:768]
    upd_ref[...] = (gate_ref[...] * out_ref[...]).reshape(8, 16, 128)
    normed, rstd = norm_rows(pair_ref[...].reshape(128, 128))
    d_normed = dot(dproj_ref[...], win_ref[...], 0, 1) + dot(dpre_ref[...], wgate_ref[...], 1, 1)
    along = jnp.mean(d_normed * normed, axis=1, keepdims=True)
    d_pair = rstd * (d_normed - jnp.mean(d_normed, axis=1, keepdims=True) - normed * along)
    dpair_ref[...] = d_pair.reshape(8, 16, 128)


def swap(values, axes):
    return lax.all_to_all(values, axes, split_axis=0, concat_axis=0, tiled=True)


def enter(pair, pair_mask, w_in, w_gate):
    held = [(128, 1, 256), (512, 128), (128, 128), (128, 128)]
    return pl.pallas_call(
        enter_kernel,
        out_shape=[jax.ShapeDtypeStruct(s, F32) for s in held],
        in_specs=[pl.BlockSpec(memory_space=pl.ANY)] * 4,
        out_specs=[pl.BlockSpec(memory_space=pl.ANY)] * 4,
        scratch_shapes=[
            pltpu.VMEM(pair.shape, F32),
            pltpu.VMEM(pair_mask.shape, pair_mask.dtype),
            pltpu.VMEM(w_in.shape, F32),
            pltpu.VMEM(w_gate.shape, F32),
            *[pltpu.VMEM(s, F32) for s in held],
            pltpu.VMEM((8, 128), F32),
            pltpu.SemaphoreType.DMA((4,)),
            pltpu.SemaphoreType.DMA((4,)),
        ],
        compiler_params=pltpu.CompilerParams(vmem_limit_bytes=60 * 1024 * 1024),
    )(pair, pair_mask, w_in, w_gate)


def shards(pair, pair_mask, w_in, w_gate, w_out, cotangent):
    msg, factor, normed, gate = enter(pair, pair_mask, w_in, w_gate)
    msg = swap(msg, CHANNELS)
    part, left, right = call(
        triangle_kernel,
        [(32, 16, 128), (256, 64), (256, 64)],
        [(2, 144, 128), (256, 64), (264, 64)],
    )(msg)
    part = swap(part, PLANE)
    (msg,) = call(home_kernel, [(16, 8, 128)], [(136, 128)])(part)
    msg = swap(msg, DEPTH)
    msg, tri = call(turn_kernel, [(16, 8, 128), (128, 128)], [(136, 128), (8, 16, 128)])(
        msg, cotangent, gate, w_out
    )
    msg = swap(msg, DEPTH)
    (d_tri,) = call(spread_kernel, [(32, 16, 128)], [(144, 128), (128, 128)])(msg)
    d_tri = swap(d_tri, PLANE)
    (msg,) = call(
        back_kernel,
        [(128, 1, 256)],
        [(256, 256), (2, 144, 128), (256, 64), (264, 64), (2, 2, 2, 4, 8, 128)],
    )(d_tri, left, right)
    msg = swap(msg, CHANNELS)
    weights, d_proj, d_pre, out_proj = call(
        weights_kernel, [(768, 128), (512, 128), (128, 128), (128, 128)]
    )(msg, factor, normed, tri, cotangent, gate, w_out)
    parts = swap(weights.reshape(32, 24, 128), PLANE)
    (parts,) = call(lambda a, b: sum_kernel(1.0, a, b), [(16, 24, 128)])(parts)
    parts = swap(parts, DEPTH)
    scale = 1.0 / (pair.shape[0] * lax.axis_size(ROW))
    (parts,) = call(lambda a, b: sum_kernel(scale, a, b), [(32, 24, 128)])(parts)
    parts = swap(parts, PLANE)
    d_pair, update, d_win, d_wgate, d_wout = call(
        leave_kernel, [(8, 16, 128), (8, 16, 128), (128, 512), (128, 128), (128, 128)]
    )(parts, d_proj, d_pre, out_proj, gate, pair, w_in, w_gate)
    return (update, d_pair, d_win, d_wgate, d_wout)


def solution(mesh):
    fine = Mesh(mesh.devices.reshape(4, 8, 4, 2, 2), ("x", "zl", "y", "zh", "co"))
    in_specs = (P(ROW, CH, None), P(ROW, CH), P(), P(), P(), P(ROW, CH, None))
    out_specs = (P(ROW, CH, None), P(ROW, CH, None), P(), P(), P())
    return jax.shard_map(shards, mesh=fine, in_specs=in_specs, out_specs=out_specs, check_vma=False)
```

```python
import jax
import jax.numpy as jnp
from jax import lax
from jax.experimental import pallas as pl
from jax.experimental.pallas import tpu as pltpu
from jax.sharding import Mesh, PartitionSpec as P

ROW = ("x", "zl")
CH = ("y", "zh", "co")
CHANNELS = ("zh", "zl", "x", "co")
PLANE = ("x", "y", "co")
DEPTH = ("zh", "zl")
F32 = jnp.float32
EPS = 1e-05


def dot(a, b, ca, cb):
    return lax.dot_general(
        a, b, (((ca,), (cb,)), ((), ())), precision=lax.Precision.HIGHEST, preferred_element_type=F32
    )


def call(body, outs, scratch=()):
    vmem = pl.BlockSpec(memory_space=pltpu.VMEM)

    def run(*args):
        return pl.pallas_call(
            body,
            out_shape=[jax.ShapeDtypeStruct(s, F32) for s in outs],
            in_specs=[vmem] * len(args),
            out_specs=[vmem] * len(outs),
            scratch_shapes=[pltpu.VMEM(s, F32) for s in scratch],
            compiler_params=pltpu.CompilerParams(vmem_limit_bytes=32 * 1024 * 1024),
        )(*args)

    return run


def norm_rows(values):
    center = values - jnp.mean(values, axis=1, keepdims=True)
    spread = jnp.mean(center * center, axis=1, keepdims=True)
    rstd = 1.0 / jnp.sqrt(spread + EPS)
    return center * rstd, rstd


def mask_lanes(mask_ref, lanes_ref):
    maskf = mask_ref[...].astype(F32)
    for ii in range(8):
        lanes_ref[0:1, ii * 16 : (ii + 1) * 16] = maskf[ii : ii + 1, :]
    return lanes_ref[0:1, :]


def enter_kernel(
    pair_hbm, mask_hbm, win_hbm, wgate_hbm, msg_hbm, factor_hbm, normed_hbm, gate_hbm,
    pair_ref, mask_ref, win_ref, wgate_ref, msg_ref, factor_ref, normed_ref, gate_ref, lanes_ref, ins, outs
):
    pairs = ((pair_hbm, pair_ref), (mask_hbm, mask_ref), (win_hbm, win_ref), (wgate_hbm, wgate_ref))
    copies = [pltpu.make_async_copy(source, target, ins.at[i]) for i, (source, target) in enumerate(pairs)]
    pairs = ((msg_ref, msg_hbm), (factor_ref, factor_hbm), (normed_ref, normed_hbm), (gate_ref, gate_hbm))
    results = [pltpu.make_async_copy(source, target, outs.at[i]) for i, (source, target) in enumerate(pairs)]
    for copy in copies:
        copy.start()
    copies[0].wait()
    normed, _ = norm_rows(pair_ref[...].reshape(128, 128))
    normed_ref[...] = normed
    results[2].start()
    copies[1].wait()
    maskf = mask_lanes(mask_ref, lanes_ref)
    copies[2].wait()
    proj = dot(win_ref[...], normed, 0, 1)
    for side in range(2):
        base = side * 256
        value = proj[base + 128 : base + 256]
        sig = jax.nn.sigmoid(proj[base : base + 128])
        masked = maskf * sig
        msg_ref[:, 0, side * 128 : (side + 1) * 128] = masked * value
        factor_ref[base : base + 128] = masked
        factor_ref[base + 128 : base + 256] = value * (1.0 - sig)
    results[0].start()
    results[1].start()
    copies[3].wait()
    gate_ref[...] = jax.nn.sigmoid(dot(normed, wgate_ref[...], 1, 0))
    results[3].start()
    for result in results:
        result.wait()


def column_blocks():
    return [
        (y * 64 + co * 32 + zh * 16, y * 64 + zh * 32 + co * 16) for y in range(4) for co in range(2) for zh in range(2)
    ]


def triangle_kernel(msg_ref, part_ref, left_ref, right_ref, flat_ref, turn_ref, natural_ref):
    flat_ref[0, 0:128] = msg_ref[:, 0, 0:128]
    flat_ref[1, 0:128] = msg_ref[:, 0, 128:256]
    for x, co, zh in channel_blocks():
        source, lanes = pl.ds(zh * 64 + x * 2 + co, 8, stride=8), slice(zh * 32 + co * 16, zh * 32 + co * 16 + 16)
        left, right = flat_ref[0, source, :], flat_ref[1, source, :]
        for s in range(8):
            left_ref[x * 64 + s * 8 : x * 64 + s * 8 + 8, lanes] = left[:, s * 16 : (s + 1) * 16]
            turn_ref[s * 32 + x * 8 : s * 32 + x * 8 + 8, lanes] = right[:, s * 16 : (s + 1) * 16]
    for s in range(8):
        natural_ref[pl.ds(s, 32, stride=8), :] = turn_ref[s * 32 : (s + 1) * 32, :]
    for to, at in column_blocks():
        right_ref[to : to + 16, :] = natural_ref[at : at + 16, :]
    part = dot(right_ref[...], left_ref[...], 1, 1)
    for x, y, co, zh in plane_blocks():
        row = y * 64 + co * 32 + zh * 16
        part_ref[(x * 4 + y) * 2 + co, :, zh * 64 : (zh + 1) * 64] = part[row : row + 16, x * 64 : (x + 1) * 64]


def channel_blocks():
    return [(x, co, zh) for x in range(4) for co in range(2) for zh in range(2)]


def plane_blocks():
    return [(x, y, co, zh) for x in range(4) for y in range(4) for co in range(2) for zh in range(2)]


def home_kernel(part_ref, msg_ref, rows_ref):
    for co in range(2):
        for x in range(4):
            at, to = x * 8 + co, (x * 2 + co) * 16
            rows_ref[to : to + 16, :] = (part_ref[at] + part_ref[at + 2]) + (part_ref[at + 4] + part_ref[at + 6])
    rows_ref[0:128] = rows_ref[0:128].T
    for zl in range(8):
        for zh in range(2):
            msg_ref[zh * 8 + zl] = rows_ref[pl.ds(zh * 64 + zl, 8, stride=8), :]


def norm_channels(values):
    center = values - jnp.mean(values, axis=0, keepdims=True)
    spread = jnp.mean(center * center, axis=0, keepdims=True)
    rstd = 1.0 / jnp.sqrt(spread + EPS)
    return center * rstd, rstd


def turn_kernel(home_ref, cot_ref, gate_ref, wout_ref, msg_ref, tri_ref, flat_ref, turn_ref):
    flat_ref[0:128] = home_ref[...].reshape(128, 128)
    for s in range(8):
        block = flat_ref[pl.ds(s, 16, stride=8), :]
        for a in range(8):
            turn_ref[a, :, s * 16 : (s + 1) * 16] = block[:, a * 16 : (a + 1) * 16]
    for a in range(8):
        flat_ref[pl.ds(a, 16, stride=8), :] = turn_ref[a]
    tri = flat_ref[0:128]
    tri_ref[...] = tri
    normed, rstd = norm_channels(tri)
    d_out = cot_ref[...].reshape(128, 128) * gate_ref[...]
    d_normed = dot(wout_ref[...], d_out, 1, 1)
    along = jnp.mean(d_normed * normed, axis=0, keepdims=True)
    flat_ref[0:128] = rstd * (d_normed - jnp.mean(d_normed, axis=0, keepdims=True) - normed * along)
    for a in range(8):
        block = flat_ref[pl.ds(a, 16, stride=8), :]
        for s in range(8):
            turn_ref[s, :, a * 16 : (a + 1) * 16] = block[:, s * 16 : (s + 1) * 16]
    for s in range(8):
        flat_ref[pl.ds(s, 16, stride=8), :] = turn_ref[s]
    msg_ref[...] = flat_ref[0:128].reshape(16, 8, 128)


def spread_kernel(msg_ref, out_ref, flat_ref, rows_ref):
    flat_ref[0:128] = msg_ref[...].reshape(128, 128)
    for zh in range(2):
        for s in range(8):
            to = zh * 64 + s * 8
            rows_ref[to : to + 8, :] = flat_ref[pl.ds(zh * 64 + s, 8, stride=8), :]
    turned = rows_ref[...].T
    for x in range(4):
        for co in range(2):
            block = turned[(x * 2 + co) * 16 : (x * 2 + co) * 16 + 16]
            for y in range(4):
                out_ref[(x * 4 + y) * 2 + co] = block


def back_kernel(
    dtri_ref, left_ref, right_ref, msg_ref, whole_ref, flat_ref, blocks_ref, natural_ref, turn_ref
):
    for x, y, co, zh in plane_blocks():
        row = y * 64 + co * 32 + zh * 16
        whole_ref[row : row + 16, x * 64 : (x + 1) * 64] = dtri_ref[
            (x * 4 + y) * 2 + co, :, zh * 64 : (zh + 1) * 64
        ]
    dtri = whole_ref[...]
    blocks_ref[...] = dot(dtri, left_ref[...], 1, 0)
    d_left = dot(right_ref[...], dtri, 0, 0).T
    for at, to in column_blocks():
        natural_ref[to : to + 16, :] = blocks_ref[at : at + 16, :]
    for s in range(8):
        d_right = natural_ref[pl.ds(s, 32, stride=8), :]
        to = slice(s * 16, (s + 1) * 16)
        for x, co, zh in channel_blocks():
            lanes = slice(zh * 32 + co * 16, zh * 32 + co * 16 + 16)
            turn_ref[0, co, zh, x, :, to] = d_left[x * 64 + s * 8 : x * 64 + s * 8 + 8, lanes]
            turn_ref[1, co, zh, x, :, to] = d_right[x * 8 : (x + 1) * 8, lanes]
    for side in range(2):
        for x, co, zh in channel_blocks():
            flat_ref[side, pl.ds(zh * 64 + x * 2 + co, 8, stride=8), :] = turn_ref[side, co, zh, x]
        msg_ref[:, 0, side * 128 : (side + 1) * 128] = flat_ref[side, 0:128]


def weights_kernel(
    msg_ref, factor_ref, normed_ref, tri_ref, cot_ref, gate_ref, wout_ref, weights_ref, dproj_ref, dpre_ref, out_ref
):
    normed = normed_ref[...]
    normed_tri, _ = norm_channels(tri_ref[...])
    gate = gate_ref[...]
    cot = cot_ref[...].reshape(128, 128)
    out_proj = dot(normed_tri, wout_ref[...], 0, 0)
    out_ref[...] = out_proj
    d_pre = cot * out_proj * gate * (1.0 - gate)
    dpre_ref[...] = d_pre
    weights_ref[512:640] = dot(normed, d_pre, 0, 0)
    weights_ref[640:768] = dot(normed_tri, cot * gate, 1, 0)
    for side in range(2):
        base = side * 256
        d_value = msg_ref[:, 0, side * 128 : (side + 1) * 128] * factor_ref[base : base + 128]
        d_gate = d_value * factor_ref[base + 128 : base + 256]
        dproj_ref[base : base + 128] = d_gate
        dproj_ref[base + 128 : base + 256] = d_value
    d_win = dot(normed, dproj_ref[...], 0, 1)
    for f in range(4):
        weights_ref[f * 128 : (f + 1) * 128] = d_win[:, f * 128 : (f + 1) * 128]


def sum_kernel(scale, parts_ref, out_ref):
    total = jnp.sum(parts_ref[...], axis=0) * scale
    for i in range(out_ref.shape[0]):
        out_ref[i] = total


def leave_kernel(
    parts_ref, dproj_ref, dpre_ref, out_ref, gate_ref, pair_ref, win_ref, wgate_ref,
    dpair_ref, upd_ref, dwin_ref, dwg_ref, dwo_ref
):
    for f in range(4):
        dwin_ref[:, f * 128 : (f + 1) * 128] = parts_ref[...].reshape(768, 128)[f * 128 : (f + 1) * 128]
    dwg_ref[...] = parts_ref[...].reshape(768, 128)[512:640]
    dwo_ref[...] = parts_ref[...].reshape(768, 128)[640:768]
    upd_ref[...] = (gate_ref[...] * out_ref[...]).reshape(8, 16, 128)
    normed, rstd = norm_rows(pair_ref[...].reshape(128, 128))
    d_normed = dot(dproj_ref[...], win_ref[...], 0, 1) + dot(dpre_ref[...], wgate_ref[...], 1, 1)
    along = jnp.mean(d_normed * normed, axis=1, keepdims=True)
    d_pair = rstd * (d_normed - jnp.mean(d_normed, axis=1, keepdims=True) - normed * along)
    dpair_ref[...] = d_pair.reshape(8, 16, 128)


def swap(values, axes):
    return lax.all_to_all(values, axes, split_axis=0, concat_axis=0, tiled=True)


def enter(pair, pair_mask, w_in, w_gate):
    held = [(128, 1, 256), (512, 128), (128, 128), (128, 128)]
    return pl.pallas_call(
        enter_kernel,
        out_shape=[jax.ShapeDtypeStruct(s, F32) for s in held],
        in_specs=[pl.BlockSpec(memory_space=pl.ANY)] * 4,
        out_specs=[pl.BlockSpec(memory_space=pl.ANY)] * 4,
        scratch_shapes=[
            pltpu.VMEM(pair.shape, F32),
            pltpu.VMEM(pair_mask.shape, pair_mask.dtype),
            pltpu.VMEM(w_in.shape, F32),
            pltpu.VMEM(w_gate.shape, F32),
            *[pltpu.VMEM(s, F32) for s in held],
            pltpu.VMEM((8, 128), F32),
            pltpu.SemaphoreType.DMA((4,)),
            pltpu.SemaphoreType.DMA((4,)),
        ],
        compiler_params=pltpu.CompilerParams(vmem_limit_bytes=60 * 1024 * 1024),
    )(pair, pair_mask, w_in, w_gate)


def shards(pair, pair_mask, w_in, w_gate, w_out, cotangent):
    msg, factor, normed, gate = enter(pair, pair_mask, w_in, w_gate)
    msg = swap(msg, CHANNELS)
    part, left, right = call(
        triangle_kernel,
        [(32, 16, 128), (256, 64), (256, 64)],
        [(2, 144, 128), (256, 64), (264, 64)],
    )(msg)
    part = swap(part, PLANE)
    (msg,) = call(home_kernel, [(16, 8, 128)], [(136, 128)])(part)
    msg = swap(msg, DEPTH)
    msg, tri = call(turn_kernel, [(16, 8, 128), (128, 128)], [(136, 128), (8, 16, 128)])(
        msg, cotangent, gate, w_out
    )
    msg = swap(msg, DEPTH)
    (d_tri,) = call(spread_kernel, [(32, 16, 128)], [(144, 128), (128, 128)])(msg)
    d_tri = swap(d_tri, PLANE)
    (msg,) = call(
        back_kernel,
        [(128, 1, 256)],
        [(256, 256), (2, 144, 128), (256, 64), (264, 64), (2, 2, 2, 4, 8, 128)],
    )(d_tri, left, right)
    msg = swap(msg, CHANNELS)
    weights, d_proj, d_pre, out_proj = call(
        weights_kernel, [(768, 128), (512, 128), (128, 128), (128, 128)]
    )(msg, factor, normed, tri, cotangent, gate, w_out)
    parts = swap(weights.reshape(32, 24, 128), PLANE)
    (parts,) = call(lambda a, b: sum_kernel(1.0, a, b), [(16, 24, 128)])(parts)
    parts = swap(parts, DEPTH)
    scale = 1.0 / (pair.shape[0] * lax.axis_size(ROW))
    (parts,) = call(lambda a, b: sum_kernel(scale, a, b), [(32, 24, 128)])(parts)
    parts = swap(parts, PLANE)
    d_pair, update, d_win, d_wgate, d_wout = call(
        leave_kernel, [(8, 16, 128), (8, 16, 128), (128, 512), (128, 128), (128, 128)]
    )(parts, d_proj, d_pre, out_proj, gate, pair, w_in, w_gate)
    return (update, d_pair, d_win, d_wgate, d_wout)


def solution(mesh):
    fine = Mesh(mesh.devices.reshape(4, 8, 4, 2, 2), ("x", "zl", "y", "zh", "co"))
    in_specs = (P(ROW, CH, None), P(ROW, CH), P(), P(), P(), P(ROW, CH, None))
    out_specs = (P(ROW, CH, None), P(ROW, CH, None), P(), P(), P())
    return jax.shard_map(shards, mesh=fine, in_specs=in_specs, out_specs=out_specs, check_vma=False)
```

```python
import jax
import jax.numpy as jnp
from jax import lax
from jax.experimental import pallas as pl
from jax.experimental.pallas import tpu as pltpu
from jax.sharding import Mesh, PartitionSpec as P

ROW = ("x", "zl")
CH = ("y", "zh", "co")
CHANNELS = ("zh", "zl", "x", "co")
PLANE = ("x", "y", "co")
DEPTH = ("zh", "zl")
F32 = jnp.float32
EPS = 1e-05


def dot(a, b, ca, cb):
    return lax.dot_general(
        a, b, (((ca,), (cb,)), ((), ())), precision=lax.Precision.HIGHEST, preferred_element_type=F32
    )


def call(body, outs, scratch=()):
    vmem = pl.BlockSpec(memory_space=pltpu.VMEM)

    def run(*args):
        return pl.pallas_call(
            body,
            out_shape=[jax.ShapeDtypeStruct(s, F32) for s in outs],
            in_specs=[vmem] * len(args),
            out_specs=[vmem] * len(outs),
            scratch_shapes=[pltpu.VMEM(s, F32) for s in scratch],
            compiler_params=pltpu.CompilerParams(vmem_limit_bytes=32 * 1024 * 1024),
        )(*args)

    return run


def norm_rows(values):
    center = values - jnp.mean(values, axis=1, keepdims=True)
    spread = jnp.mean(center * center, axis=1, keepdims=True)
    rstd = 1.0 / jnp.sqrt(spread + EPS)
    return center * rstd, rstd


def mask_lanes(mask_ref, lanes_ref):
    maskf = mask_ref[...].astype(F32)
    for ii in range(8):
        lanes_ref[0:1, ii * 16 : (ii + 1) * 16] = maskf[ii : ii + 1, :]
    return lanes_ref[0:1, :]


def enter_kernel(
    pair_hbm, mask_hbm, win_hbm, wgate_hbm, msg_hbm, factor_hbm, normed_hbm, gate_hbm,
    pair_ref, mask_ref, win_ref, wgate_ref, msg_ref, factor_ref, normed_ref, gate_ref, lanes_ref, ins, outs
):
    pairs = ((pair_hbm, pair_ref), (mask_hbm, mask_ref), (win_hbm, win_ref), (wgate_hbm, wgate_ref))
    copies = [pltpu.make_async_copy(source, target, ins.at[i]) for i, (source, target) in enumerate(pairs)]
    pairs = ((msg_ref, msg_hbm), (factor_ref, factor_hbm), (normed_ref, normed_hbm), (gate_ref, gate_hbm))
    results = [pltpu.make_async_copy(source, target, outs.at[i]) for i, (source, target) in enumerate(pairs)]
    for copy in copies:
        copy.start()
    copies[0].wait()
    normed, _ = norm_rows(pair_ref[...].reshape(128, 128))
    normed_ref[...] = normed
    results[2].start()
    copies[1].wait()
    maskf = mask_lanes(mask_ref, lanes_ref)
    copies[2].wait()
    for side in range(2):
        base = side * 256
        proj = dot(win_ref[:, base : base + 256], normed, 0, 1)
        value = proj[128:256]
        sig = jax.nn.sigmoid(proj[0:128])
        masked = maskf * sig
        msg_ref[:, 0, side * 128 : (side + 1) * 128] = masked * value
        factor_ref[base : base + 128] = masked
        factor_ref[base + 128 : base + 256] = value * (1.0 - sig)
    results[0].start()
    results[1].start()
    copies[3].wait()
    gate_ref[...] = jax.nn.sigmoid(dot(normed, wgate_ref[...], 1, 0))
    results[3].start()
    for result in results:
        result.wait()


def column_blocks():
    return [
        ((y * 2 + co) * 16, zh * 64, y * 64 + zh * 32 + co * 16)
        for y in range(4) for co in range(2) for zh in range(2)
    ]


def channel_blocks():
    return [(x, co, zh) for x in range(4) for co in range(2) for zh in range(2)]


def triangle_kernel(msg_ref, part_ref, left_ref, right_ref, flat_ref, rows_ref, turn_ref, natural_ref):
    flat_ref[0, 0:128] = msg_ref[:, 0, 0:128]
    flat_ref[1, 0:128] = msg_ref[:, 0, 128:256]
    for x, co, zh in channel_blocks():
        source, lanes = pl.ds(zh * 64 + x * 2 + co, 8, stride=8), slice(zh * 32 + co * 16, zh * 32 + co * 16 + 16)
        left, right = flat_ref[0, source, :], flat_ref[1, source, :]
        for s in range(8):
            rows_ref[x * 64 + s * 8 : x * 64 + s * 8 + 8, lanes] = left[:, s * 16 : (s + 1) * 16]
            turn_ref[s * 32 + x * 8 : s * 32 + x * 8 + 8, lanes] = right[:, s * 16 : (s + 1) * 16]
    for s in range(8):
        natural_ref[pl.ds(s, 32, stride=8), :] = turn_ref[s * 32 : (s + 1) * 32, :]
    for row, lane, at in column_blocks():
        right_ref[row : row + 16, lane : lane + 64] = natural_ref[at : at + 16, :]
    left_ref[...] = jnp.zeros((512, 128), F32)
    for x in range(4):
        block = rows_ref[x * 64 : (x + 1) * 64, :]
        left_ref[x * 128 : x * 128 + 64, 0:64] = block
        left_ref[x * 128 + 64 : x * 128 + 128, 64:128] = block
    part = dot(right_ref[...], left_ref[...], 1, 1)
    for x in range(4):
        part_ref[x * 8 : (x + 1) * 8] = part[:, x * 128 : (x + 1) * 128].reshape(8, 16, 128)


def home_kernel(part_ref, msg_ref, rows_ref):
    for co in range(2):
        for x in range(4):
            at, to = x * 8 + co, (x * 2 + co) * 16
            rows_ref[to : to + 16, :] = (part_ref[at] + part_ref[at + 2]) + (part_ref[at + 4] + part_ref[at + 6])
    rows_ref[0:128] = rows_ref[0:128].T
    for zl in range(8):
        for zh in range(2):
            msg_ref[zh * 8 + zl] = rows_ref[pl.ds(zh * 64 + zl, 8, stride=8), :]


def norm_channels(values):
    center = values - jnp.mean(values, axis=0, keepdims=True)
    spread = jnp.mean(center * center, axis=0, keepdims=True)
    rstd = 1.0 / jnp.sqrt(spread + EPS)
    return center * rstd, rstd


def turn_kernel(home_ref, cot_ref, gate_ref, wout_ref, msg_ref, tri_ref, flat_ref, turn_ref):
    flat_ref[0:128] = home_ref[...].reshape(128, 128)
    for s in range(8):
        block = flat_ref[pl.ds(s, 16, stride=8), :]
        for a in range(8):
            turn_ref[a, :, s * 16 : (s + 1) * 16] = block[:, a * 16 : (a + 1) * 16]
    for a in range(8):
        flat_ref[pl.ds(a, 16, stride=8), :] = turn_ref[a]
    tri = flat_ref[0:128]
    tri_ref[...] = tri
    normed, rstd = norm_channels(tri)
    d_out = cot_ref[...].reshape(128, 128) * gate_ref[...]
    d_normed = dot(wout_ref[...], d_out, 1, 1)
    along = jnp.mean(d_normed * normed, axis=0, keepdims=True)
    flat_ref[0:128] = rstd * (d_normed - jnp.mean(d_normed, axis=0, keepdims=True) - normed * along)
    for a in range(8):
        block = flat_ref[pl.ds(a, 16, stride=8), :]
        for s in range(8):
            turn_ref[s, :, a * 16 : (a + 1) * 16] = block[:, s * 16 : (s + 1) * 16]
    for s in range(8):
        flat_ref[pl.ds(s, 16, stride=8), :] = turn_ref[s]
    msg_ref[...] = flat_ref[0:128].reshape(16, 8, 128)


def spread_kernel(msg_ref, out_ref, flat_ref, rows_ref):
    flat_ref[0:128] = msg_ref[...].reshape(128, 128)
    for zh in range(2):
        for s in range(8):
            to = zh * 64 + s * 8
            rows_ref[to : to + 8, :] = flat_ref[pl.ds(zh * 64 + s, 8, stride=8), :]
    turned = rows_ref[...].T
    for x in range(4):
        for co in range(2):
            block = turned[(x * 2 + co) * 16 : (x * 2 + co) * 16 + 16]
            for y in range(4):
                out_ref[(x * 4 + y) * 2 + co] = block


def back_kernel(dtri_ref, left_ref, right_ref, msg_ref, flat_ref, rows_ref, natural_ref, turn_ref):
    right = right_ref[...]
    total = jnp.zeros((128, 128), F32)
    for x in range(4):
        block = dtri_ref[x * 8 : (x + 1) * 8].reshape(128, 128)
        total += dot(block, left_ref[x * 128 : (x + 1) * 128], 1, 0)
        both = dot(block, right, 0, 0)
        rows_ref[x * 64 : (x + 1) * 64, :] = both[0:64, 0:64] + both[64:128, 64:128]
    for row, lane, at in column_blocks():
        natural_ref[at : at + 16, :] = total[row : row + 16, lane : lane + 64]
    for s in range(8):
        d_right = natural_ref[pl.ds(s, 32, stride=8), :]
        to = slice(s * 16, (s + 1) * 16)
        for x, co, zh in channel_blocks():
            lanes = slice(zh * 32 + co * 16, zh * 32 + co * 16 + 16)
            turn_ref[0, co, zh, x, :, to] = rows_ref[x * 64 + s * 8 : x * 64 + s * 8 + 8, lanes]
            turn_ref[1, co, zh, x, :, to] = d_right[x * 8 : (x + 1) * 8, lanes]
    for side in range(2):
        for x, co, zh in channel_blocks():
            flat_ref[side, pl.ds(zh * 64 + x * 2 + co, 8, stride=8), :] = turn_ref[side, co, zh, x]
        msg_ref[:, 0, side * 128 : (side + 1) * 128] = flat_ref[side, 0:128]


def weights_kernel(
    msg_ref, factor_ref, normed_ref, tri_ref, cot_ref, gate_ref, wout_ref, weights_ref, dproj_ref, dpre_ref, out_ref
):
    normed = normed_ref[...]
    normed_tri, _ = norm_channels(tri_ref[...])
    gate = gate_ref[...]
    cot = cot_ref[...].reshape(128, 128)
    out_proj = dot(normed_tri, wout_ref[...], 0, 0)
    out_ref[...] = out_proj
    d_pre = cot * out_proj * gate * (1.0 - gate)
    dpre_ref[...] = d_pre
    weights_ref[512:640] = dot(normed, d_pre, 0, 0)
    weights_ref[640:768] = dot(normed_tri, cot * gate, 1, 0)
    for side in range(2):
        base = side * 256
        d_value = msg_ref[:, 0, side * 128 : (side + 1) * 128] * factor_ref[base : base + 128]
        d_gate = d_value * factor_ref[base + 128 : base + 256]
        dproj_ref[base : base + 128] = d_gate
        dproj_ref[base + 128 : base + 256] = d_value
    d_win = dot(normed, dproj_ref[...], 0, 1)
    for f in range(4):
        weights_ref[f * 128 : (f + 1) * 128] = d_win[:, f * 128 : (f + 1) * 128]


def sum_kernel(scale, parts_ref, out_ref):
    total = jnp.sum(parts_ref[...], axis=0) * scale
    for i in range(out_ref.shape[0]):
        out_ref[i] = total


def leave_kernel(
    parts_ref, dproj_ref, dpre_ref, out_ref, gate_ref, pair_ref, win_ref, wgate_ref,
    dpair_hbm, upd_hbm, dwin_hbm, dwg_hbm, dwo_hbm, dpair_ref, upd_ref, sems
):
    pairs = [
        (parts_ref.at[pl.ds(f * 128, 128), :], dwin_hbm.at[:, pl.ds(f * 128, 128)]) for f in range(4)
    ]
    pairs += [(parts_ref.at[pl.ds(512, 128), :], dwg_hbm), (parts_ref.at[pl.ds(640, 128), :], dwo_hbm)]
    pairs += [(upd_ref, upd_hbm), (dpair_ref, dpair_hbm)]
    copies = [pltpu.make_async_copy(source, target, sems.at[i]) for i, (source, target) in enumerate(pairs)]
    for copy in copies[:6]:
        copy.start()
    upd_ref[...] = (gate_ref[...] * out_ref[...]).reshape(8, 16, 128)
    copies[6].start()
    normed, rstd = norm_rows(pair_ref[...].reshape(128, 128))
    d_normed = dot(dproj_ref[...], win_ref[...], 0, 1) + dot(dpre_ref[...], wgate_ref[...], 1, 1)
    along = jnp.mean(d_normed * normed, axis=1, keepdims=True)
    d_pair = rstd * (d_normed - jnp.mean(d_normed, axis=1, keepdims=True) - normed * along)
    dpair_ref[...] = d_pair.reshape(8, 16, 128)
    copies[7].start()
    for copy in copies:
        copy.wait()


def swap(values, axes):
    return lax.all_to_all(values, axes, split_axis=0, concat_axis=0, tiled=True)


def enter(pair, pair_mask, w_in, w_gate):
    held = [(128, 1, 256), (512, 128), (128, 128), (128, 128)]
    return pl.pallas_call(
        enter_kernel,
        out_shape=[jax.ShapeDtypeStruct(s, F32) for s in held],
        in_specs=[pl.BlockSpec(memory_space=pl.ANY)] * 4,
        out_specs=[pl.BlockSpec(memory_space=pl.ANY)] * 4,
        scratch_shapes=[
            pltpu.VMEM(pair.shape, F32),
            pltpu.VMEM(pair_mask.shape, pair_mask.dtype),
            pltpu.VMEM(w_in.shape, F32),
            pltpu.VMEM(w_gate.shape, F32),
            *[pltpu.VMEM(s, F32) for s in held],
            pltpu.VMEM((8, 128), F32),
            pltpu.SemaphoreType.DMA((4,)),
            pltpu.SemaphoreType.DMA((4,)),
        ],
        compiler_params=pltpu.CompilerParams(vmem_limit_bytes=60 * 1024 * 1024),
    )(pair, pair_mask, w_in, w_gate)


def leave(*args):
    outs = [(8, 16, 128), (8, 16, 128), (128, 512), (128, 128), (128, 128)]
    return pl.pallas_call(
        leave_kernel,
        out_shape=[jax.ShapeDtypeStruct(s, F32) for s in outs],
        in_specs=[pl.BlockSpec(memory_space=pltpu.VMEM)] * len(args),
        out_specs=[pl.BlockSpec(memory_space=pl.ANY)] * len(outs),
        scratch_shapes=[pltpu.VMEM(outs[0], F32), pltpu.VMEM(outs[1], F32), pltpu.SemaphoreType.DMA((8,))],
        compiler_params=pltpu.CompilerParams(vmem_limit_bytes=32 * 1024 * 1024),
    )(*args)


def shards(pair, pair_mask, w_in, w_gate, w_out, cotangent):
    msg, factor, normed, gate = enter(pair, pair_mask, w_in, w_gate)
    msg = swap(msg, CHANNELS)
    part, left, right = call(
        triangle_kernel,
        [(32, 16, 128), (512, 128), (128, 128)],
        [(2, 144, 128), (256, 64), (256, 64), (264, 64)],
    )(msg)
    part = swap(part, PLANE)
    (msg,) = call(home_kernel, [(16, 8, 128)], [(136, 128)])(part)
    msg = swap(msg, DEPTH)
    msg, tri = call(turn_kernel, [(16, 8, 128), (128, 128)], [(136, 128), (8, 16, 128)])(
        msg, cotangent, gate, w_out
    )
    msg = swap(msg, DEPTH)
    (d_tri,) = call(spread_kernel, [(32, 16, 128)], [(144, 128), (128, 128)])(msg)
    d_tri = swap(d_tri, PLANE)
    (msg,) = call(
        back_kernel,
        [(128, 1, 256)],
        [(2, 144, 128), (256, 64), (264, 64), (2, 2, 2, 4, 8, 128)],
    )(d_tri, left, right)
    msg = swap(msg, CHANNELS)
    weights, d_proj, d_pre, out_proj = call(
        weights_kernel, [(768, 128), (512, 128), (128, 128), (128, 128)]
    )(msg, factor, normed, tri, cotangent, gate, w_out)
    parts = swap(weights.reshape(32, 24, 128), PLANE)
    (parts,) = call(lambda a, b: sum_kernel(1.0, a, b), [(16, 24, 128)])(parts)
    parts = swap(parts, DEPTH)
    scale = 1.0 / (pair.shape[0] * lax.axis_size(ROW))
    (parts,) = call(lambda a, b: sum_kernel(scale, a, b), [(32, 24, 128)])(parts)
    parts = swap(parts, PLANE)
    d_pair, update, d_win, d_wgate, d_wout = leave(
        parts.reshape(768, 128), d_proj, d_pre, out_proj, gate, pair, w_in, w_gate
    )
    return (update, d_pair, d_win, d_wgate, d_wout)


def solution(mesh):
    fine = Mesh(mesh.devices.reshape(4, 8, 4, 2, 2), ("x", "zl", "y", "zh", "co"))
    in_specs = (P(ROW, CH, None), P(ROW, CH), P(), P(), P(), P(ROW, CH, None))
    out_specs = (P(ROW, CH, None), P(ROW, CH, None), P(), P(), P())
    return jax.shard_map(shards, mesh=fine, in_specs=in_specs, out_specs=out_specs, check_vma=False)
```

```python
import jax
import jax.numpy as jnp
from jax import lax
from jax.experimental import pallas as pl
from jax.experimental.pallas import tpu as pltpu
from jax.sharding import Mesh, PartitionSpec as P

ROW = ("x", "zl")
CH = ("y", "zh", "co")
CHANNELS = ("zh", "zl", "x", "co")
PLANE = ("x", "y", "co")
DEPTH = ("zh", "zl")
F32 = jnp.float32
EPS = 1e-05


def dot(a, b, ca, cb):
    return lax.dot_general(
        a, b, (((ca,), (cb,)), ((), ())), precision=lax.Precision.HIGHEST, preferred_element_type=F32
    )


def call(body, outs, scratch=()):
    vmem = pl.BlockSpec(memory_space=pltpu.VMEM)

    def run(*args):
        return pl.pallas_call(
            body,
            out_shape=[jax.ShapeDtypeStruct(s, F32) for s in outs],
            in_specs=[vmem] * len(args),
            out_specs=[vmem] * len(outs),
            scratch_shapes=[pltpu.VMEM(s, F32) for s in scratch],
            compiler_params=pltpu.CompilerParams(vmem_limit_bytes=32 * 1024 * 1024),
        )(*args)

    return run


def norm_rows(values):
    center = values - jnp.mean(values, axis=1, keepdims=True)
    spread = jnp.mean(center * center, axis=1, keepdims=True)
    rstd = 1.0 / jnp.sqrt(spread + EPS)
    return center * rstd, rstd


def mask_lanes(mask_ref, lanes_ref):
    maskf = mask_ref[...].astype(F32)
    for ii in range(8):
        lanes_ref[0:1, ii * 16 : (ii + 1) * 16] = maskf[ii : ii + 1, :]
    return lanes_ref[0:1, :]


def clear_kernel(lanes_ref):
    lanes_ref[...] = jnp.zeros((8, 128), F32)


def enter_kernel(
    lanes_in, pair_ref, mask_ref, win_ref, wgate_ref, msg_ref, factor_ref, normed_ref, gate_ref, lanes_ref
):
    lanes_ref[...] = lanes_in[...]
    normed, _ = norm_rows(pair_ref[...].reshape(128, 128))
    normed_ref[...] = normed
    maskf = mask_lanes(mask_ref, lanes_ref)
    for side in range(2):
        base = side * 256
        proj = dot(win_ref[:, base : base + 256], normed, 0, 1)
        value = proj[128:256]
        sig = jax.nn.sigmoid(proj[0:128])
        masked = maskf * sig
        msg_ref[:, 0, side * 128 : (side + 1) * 128] = masked * value
        factor_ref[base : base + 128] = masked
        factor_ref[base + 128 : base + 256] = value * (1.0 - sig)
    gate_ref[...] = jax.nn.sigmoid(dot(normed, wgate_ref[...], 1, 0))


def column_blocks():
    return [
        ((y * 2 + co) * 16, zh * 64, y * 64 + zh * 32 + co * 16)
        for y in range(4) for co in range(2) for zh in range(2)
    ]


def channel_blocks():
    return [(x, co, zh) for x in range(4) for co in range(2) for zh in range(2)]


def triangle_kernel(msg_ref, part_ref, left_ref, right_ref, flat_ref, rows_ref, turn_ref, natural_ref):
    flat_ref[0, 0:128] = msg_ref[:, 0, 0:128]
    flat_ref[1, 0:128] = msg_ref[:, 0, 128:256]
    for x, co, zh in channel_blocks():
        source, lanes = pl.ds(zh * 64 + x * 2 + co, 8, stride=8), slice(zh * 32 + co * 16, zh * 32 + co * 16 + 16)
        left, right = flat_ref[0, source, :], flat_ref[1, source, :]
        for s in range(8):
            rows_ref[x * 64 + s * 8 : x * 64 + s * 8 + 8, lanes] = left[:, s * 16 : (s + 1) * 16]
            turn_ref[s * 32 + x * 8 : s * 32 + x * 8 + 8, lanes] = right[:, s * 16 : (s + 1) * 16]
    for s in range(8):
        natural_ref[pl.ds(s, 32, stride=8), :] = turn_ref[s * 32 : (s + 1) * 32, :]
    for row, lane, at in column_blocks():
        right_ref[row : row + 16, lane : lane + 64] = natural_ref[at : at + 16, :]
    left_ref[...] = jnp.zeros((512, 128), F32)
    for x in range(4):
        block = rows_ref[x * 64 : (x + 1) * 64, :]
        left_ref[x * 128 : x * 128 + 64, 0:64] = block
        left_ref[x * 128 + 64 : x * 128 + 128, 64:128] = block
    part = dot(right_ref[...], left_ref[...], 1, 1)
    for x in range(4):
        part_ref[x * 8 : (x + 1) * 8] = part[:, x * 128 : (x + 1) * 128].reshape(8, 16, 128)


def home_kernel(part_ref, msg_ref, rows_ref):
    for co in range(2):
        for x in range(4):
            at, to = x * 8 + co, (x * 2 + co) * 16
            rows_ref[to : to + 16, :] = (part_ref[at] + part_ref[at + 2]) + (part_ref[at + 4] + part_ref[at + 6])
    rows_ref[0:128] = rows_ref[0:128].T
    for zl in range(8):
        for zh in range(2):
            msg_ref[zh * 8 + zl] = rows_ref[pl.ds(zh * 64 + zl, 8, stride=8), :]


def norm_channels(values):
    center = values - jnp.mean(values, axis=0, keepdims=True)
    spread = jnp.mean(center * center, axis=0, keepdims=True)
    rstd = 1.0 / jnp.sqrt(spread + EPS)
    return center * rstd, rstd


def turn_kernel(home_ref, cot_ref, gate_ref, wout_ref, msg_ref, tri_ref, flat_ref, turn_ref):
    flat_ref[0:128] = home_ref[...].reshape(128, 128)
    for s in range(8):
        block = flat_ref[pl.ds(s, 16, stride=8), :]
        for a in range(8):
            turn_ref[a, :, s * 16 : (s + 1) * 16] = block[:, a * 16 : (a + 1) * 16]
    for a in range(8):
        flat_ref[pl.ds(a, 16, stride=8), :] = turn_ref[a]
    tri = flat_ref[0:128]
    tri_ref[...] = tri
    normed, rstd = norm_channels(tri)
    d_out = cot_ref[...].reshape(128, 128) * gate_ref[...]
    d_normed = dot(wout_ref[...], d_out, 1, 1)
    along = jnp.mean(d_normed * normed, axis=0, keepdims=True)
    flat_ref[0:128] = rstd * (d_normed - jnp.mean(d_normed, axis=0, keepdims=True) - normed * along)
    for a in range(8):
        block = flat_ref[pl.ds(a, 16, stride=8), :]
        for s in range(8):
            turn_ref[s, :, a * 16 : (a + 1) * 16] = block[:, s * 16 : (s + 1) * 16]
    for s in range(8):
        flat_ref[pl.ds(s, 16, stride=8), :] = turn_ref[s]
    msg_ref[...] = flat_ref[0:128].reshape(16, 8, 128)


def spread_kernel(msg_ref, out_ref, flat_ref, rows_ref):
    flat_ref[0:128] = msg_ref[...].reshape(128, 128)
    for zh in range(2):
        for s in range(8):
            to = zh * 64 + s * 8
            rows_ref[to : to + 8, :] = flat_ref[pl.ds(zh * 64 + s, 8, stride=8), :]
    turned = rows_ref[...].T
    for x in range(4):
        for co in range(2):
            block = turned[(x * 2 + co) * 16 : (x * 2 + co) * 16 + 16]
            for y in range(4):
                out_ref[(x * 4 + y) * 2 + co] = block


def back_kernel(dtri_ref, left_ref, right_ref, msg_ref, flat_ref, rows_ref, natural_ref, turn_ref):
    right = right_ref[...]
    total = jnp.zeros((128, 128), F32)
    for x in range(4):
        block = dtri_ref[x * 8 : (x + 1) * 8].reshape(128, 128)
        total += dot(block, left_ref[x * 128 : (x + 1) * 128], 1, 0)
        both = dot(block, right, 0, 0)
        rows_ref[x * 64 : (x + 1) * 64, :] = both[0:64, 0:64] + both[64:128, 64:128]
    for row, lane, at in column_blocks():
        natural_ref[at : at + 16, :] = total[row : row + 16, lane : lane + 64]
    for s in range(8):
        d_right = natural_ref[pl.ds(s, 32, stride=8), :]
        to = slice(s * 16, (s + 1) * 16)
        for x, co, zh in channel_blocks():
            lanes = slice(zh * 32 + co * 16, zh * 32 + co * 16 + 16)
            turn_ref[0, co, zh, x, :, to] = rows_ref[x * 64 + s * 8 : x * 64 + s * 8 + 8, lanes]
            turn_ref[1, co, zh, x, :, to] = d_right[x * 8 : (x + 1) * 8, lanes]
    for side in range(2):
        for x, co, zh in channel_blocks():
            flat_ref[side, pl.ds(zh * 64 + x * 2 + co, 8, stride=8), :] = turn_ref[side, co, zh, x]
        msg_ref[:, 0, side * 128 : (side + 1) * 128] = flat_ref[side, 0:128]


def weights_kernel(
    msg_ref, factor_ref, normed_ref, tri_ref, cot_ref, gate_ref, wout_ref, weights_ref, dproj_ref, dpre_ref, out_ref
):
    normed = normed_ref[...]
    normed_tri, _ = norm_channels(tri_ref[...])
    gate = gate_ref[...]
    cot = cot_ref[...].reshape(128, 128)
    out_proj = dot(normed_tri, wout_ref[...], 0, 0)
    out_ref[...] = out_proj
    d_pre = cot * out_proj * gate * (1.0 - gate)
    dpre_ref[...] = d_pre
    weights_ref[512:640] = dot(normed, d_pre, 0, 0)
    weights_ref[640:768] = dot(normed_tri, cot * gate, 1, 0)
    for side in range(2):
        base = side * 256
        d_value = msg_ref[:, 0, side * 128 : (side + 1) * 128] * factor_ref[base : base + 128]
        d_gate = d_value * factor_ref[base + 128 : base + 256]
        dproj_ref[base : base + 128] = d_gate
        dproj_ref[base + 128 : base + 256] = d_value
    d_win = dot(normed, dproj_ref[...], 0, 1)
    for f in range(4):
        weights_ref[f * 128 : (f + 1) * 128] = d_win[:, f * 128 : (f + 1) * 128]


def sum_kernel(scale, parts_ref, out_ref):
    total = jnp.sum(parts_ref[...], axis=0) * scale
    for i in range(out_ref.shape[0]):
        out_ref[i] = total


def leave_kernel(
    parts_ref, dproj_ref, dpre_ref, out_ref, gate_ref, pair_ref, win_ref, wgate_ref,
    dpair_hbm, upd_hbm, dwin_hbm, dwg_hbm, dwo_hbm, dpair_ref, upd_ref, sems
):
    pairs = [
        (parts_ref.at[pl.ds(f * 128, 128), :], dwin_hbm.at[:, pl.ds(f * 128, 128)]) for f in range(4)
    ]
    pairs += [(parts_ref.at[pl.ds(512, 128), :], dwg_hbm), (parts_ref.at[pl.ds(640, 128), :], dwo_hbm)]
    pairs += [(upd_ref, upd_hbm), (dpair_ref, dpair_hbm)]
    copies = [pltpu.make_async_copy(source, target, sems.at[i]) for i, (source, target) in enumerate(pairs)]
    for copy in copies[:6]:
        copy.start()
    upd_ref[...] = (gate_ref[...] * out_ref[...]).reshape(8, 16, 128)
    copies[6].start()
    normed, rstd = norm_rows(pair_ref[...].reshape(128, 128))
    d_normed = dot(dproj_ref[...], win_ref[...], 0, 1) + dot(dpre_ref[...], wgate_ref[...], 1, 1)
    along = jnp.mean(d_normed * normed, axis=1, keepdims=True)
    d_pair = rstd * (d_normed - jnp.mean(d_normed, axis=1, keepdims=True) - normed * along)
    dpair_ref[...] = d_pair.reshape(8, 16, 128)
    copies[7].start()
    for copy in copies:
        copy.wait()


def swap(values, axes):
    return lax.all_to_all(values, axes, split_axis=0, concat_axis=0, tiled=True)


def enter(pair, pair_mask, w_in, w_gate):
    lanes = pl.pallas_call(
        clear_kernel,
        out_shape=jax.ShapeDtypeStruct((8, 128), F32),
        out_specs=pl.BlockSpec(memory_space=pltpu.VMEM),
        cost_estimate=pl.CostEstimate(flops=10**10, bytes_accessed=2**25, transcendentals=0),
        compiler_params=pltpu.CompilerParams(vmem_limit_bytes=4 * 1024 * 1024),
    )()
    held = [(128, 1, 256), (512, 128), (128, 128), (128, 128)]
    return call(enter_kernel, held, [(8, 128)])(lanes, pair, pair_mask, w_in, w_gate)


def leave(*args):
    outs = [(8, 16, 128), (8, 16, 128), (128, 512), (128, 128), (128, 128)]
    return pl.pallas_call(
        leave_kernel,
        out_shape=[jax.ShapeDtypeStruct(s, F32) for s in outs],
        in_specs=[pl.BlockSpec(memory_space=pltpu.VMEM)] * len(args),
        out_specs=[pl.BlockSpec(memory_space=pl.ANY)] * len(outs),
        scratch_shapes=[pltpu.VMEM(outs[0], F32), pltpu.VMEM(outs[1], F32), pltpu.SemaphoreType.DMA((8,))],
        compiler_params=pltpu.CompilerParams(vmem_limit_bytes=32 * 1024 * 1024),
    )(*args)


def shards(pair, pair_mask, w_in, w_gate, w_out, cotangent):
    msg, factor, normed, gate = enter(pair, pair_mask, w_in, w_gate)
    msg = swap(msg, CHANNELS)
    part, left, right = call(
        triangle_kernel,
        [(32, 16, 128), (512, 128), (128, 128)],
        [(2, 144, 128), (256, 64), (256, 64), (264, 64)],
    )(msg)
    part = swap(part, PLANE)
    (msg,) = call(home_kernel, [(16, 8, 128)], [(136, 128)])(part)
    msg = swap(msg, DEPTH)
    msg, tri = call(turn_kernel, [(16, 8, 128), (128, 128)], [(136, 128), (8, 16, 128)])(
        msg, cotangent, gate, w_out
    )
    msg = swap(msg, DEPTH)
    (d_tri,) = call(spread_kernel, [(32, 16, 128)], [(144, 128), (128, 128)])(msg)
    d_tri = swap(d_tri, PLANE)
    (msg,) = call(
        back_kernel,
        [(128, 1, 256)],
        [(2, 144, 128), (256, 64), (264, 64), (2, 2, 2, 4, 8, 128)],
    )(d_tri, left, right)
    msg = swap(msg, CHANNELS)
    weights, d_proj, d_pre, out_proj = call(
        weights_kernel, [(768, 128), (512, 128), (128, 128), (128, 128)]
    )(msg, factor, normed, tri, cotangent, gate, w_out)
    parts = swap(weights.reshape(32, 24, 128), PLANE)
    (parts,) = call(lambda a, b: sum_kernel(1.0, a, b), [(16, 24, 128)])(parts)
    parts = swap(parts, DEPTH)
    scale = 1.0 / (pair.shape[0] * lax.axis_size(ROW))
    (parts,) = call(lambda a, b: sum_kernel(scale, a, b), [(32, 24, 128)])(parts)
    parts = swap(parts, PLANE)
    d_pair, update, d_win, d_wgate, d_wout = leave(
        parts.reshape(768, 128), d_proj, d_pre, out_proj, gate, pair, w_in, w_gate
    )
    return (update, d_pair, d_win, d_wgate, d_wout)


def solution(mesh):
    fine = Mesh(mesh.devices.reshape(4, 8, 4, 2, 2), ("x", "zl", "y", "zh", "co"))
    in_specs = (P(ROW, CH, None), P(ROW, CH), P(), P(), P(), P(ROW, CH, None))
    out_specs = (P(ROW, CH, None), P(ROW, CH, None), P(), P(), P())
    return jax.shard_map(shards, mesh=fine, in_specs=in_specs, out_specs=out_specs, check_vma=False)
```

```python
import jax
import jax.numpy as jnp
from jax import lax
from jax.experimental import pallas as pl
from jax.experimental.pallas import tpu as pltpu
from jax.sharding import Mesh, PartitionSpec as P

ROW = ("x", "zl")
CH = ("y", "zh", "co")
CHANNELS = ("zh", "zl", "x", "co")
PLANE = ("x", "y", "co")
DEPTH = ("zh", "zl")
F32 = jnp.float32
EPS = 1e-05


def dot(a, b, ca, cb):
    return lax.dot_general(
        a, b, (((ca,), (cb,)), ((), ())), precision=lax.Precision.HIGHEST, preferred_element_type=F32
    )


def call(body, outs, scratch=()):
    vmem = pl.BlockSpec(memory_space=pltpu.VMEM)

    def run(*args):
        return pl.pallas_call(
            body,
            out_shape=[jax.ShapeDtypeStruct(s, F32) for s in outs],
            in_specs=[vmem] * len(args),
            out_specs=[vmem] * len(outs),
            scratch_shapes=[pltpu.VMEM(s, F32) for s in scratch],
            compiler_params=pltpu.CompilerParams(vmem_limit_bytes=32 * 1024 * 1024),
        )(*args)

    return run


def norm_rows(values):
    center = values - jnp.mean(values, axis=1, keepdims=True)
    spread = jnp.mean(center * center, axis=1, keepdims=True)
    rstd = 1.0 / jnp.sqrt(spread + EPS)
    return center * rstd, rstd


def mask_lanes(mask_ref, lanes_ref):
    maskf = mask_ref[...].astype(F32)
    for ii in range(8):
        lanes_ref[0:1, ii * 16 : (ii + 1) * 16] = maskf[ii : ii + 1, :]
    return lanes_ref[0:1, :]


def clear_kernel(lanes_ref):
    lanes_ref[...] = jnp.zeros((8, 128), F32)


def enter_kernel(
    lanes_in, pair_ref, mask_ref, win_ref, wgate_ref, msg_ref, factor_ref, normed_ref, gate_ref, lanes_ref
):
    lanes_ref[...] = lanes_in[...]
    normed, _ = norm_rows(pair_ref[...].reshape(128, 128))
    normed_ref[...] = normed
    maskf = mask_lanes(mask_ref, lanes_ref)
    for side in range(2):
        base = side * 256
        proj = dot(win_ref[:, base : base + 256], normed, 0, 1)
        value = proj[128:256]
        sig = jax.nn.sigmoid(proj[0:128])
        masked = maskf * sig
        msg_ref[:, side, :] = masked * value
        factor_ref[base : base + 128] = masked
        factor_ref[base + 128 : base + 256] = value * (1.0 - sig)
    gate_ref[...] = jax.nn.sigmoid(dot(normed, wgate_ref[...], 1, 0))


def column_blocks():
    return [
        ((y * 2 + co) * 16, zh * 64, y * 64 + zh * 32 + co * 16)
        for y in range(4) for co in range(2) for zh in range(2)
    ]


def channel_blocks():
    return [(x, co, zh) for x in range(4) for co in range(2) for zh in range(2)]


def triangle_kernel(msg_ref, part_ref, left_ref, right_ref, rows_ref, turn_ref, natural_ref):
    for x, co, zh in channel_blocks():
        source, lanes = pl.ds(zh * 64 + x * 2 + co, 8, stride=8), slice(zh * 32 + co * 16, zh * 32 + co * 16 + 16)
        left, right = msg_ref[source, 0, :], msg_ref[source, 1, :]
        for s in range(8):
            rows_ref[x * 64 + s * 8 : x * 64 + s * 8 + 8, lanes] = left[:, s * 16 : (s + 1) * 16]
            turn_ref[s * 32 + x * 8 : s * 32 + x * 8 + 8, lanes] = right[:, s * 16 : (s + 1) * 16]
    for s in range(8):
        natural_ref[pl.ds(s, 32, stride=8), :] = turn_ref[s * 32 : (s + 1) * 32, :]
    for row, lane, at in column_blocks():
        right_ref[row : row + 16, lane : lane + 64] = natural_ref[at : at + 16, :]
    left_ref[...] = jnp.zeros((512, 128), F32)
    for x in range(4):
        block = rows_ref[x * 64 : (x + 1) * 64, :]
        left_ref[x * 128 : x * 128 + 64, 0:64] = block
        left_ref[x * 128 + 64 : x * 128 + 128, 64:128] = block
    part = dot(right_ref[...], left_ref[...], 1, 1)
    for x in range(4):
        part_ref[x * 8 : (x + 1) * 8] = part[:, x * 128 : (x + 1) * 128].reshape(8, 16, 128)


def home_kernel(part_ref, msg_ref, rows_ref):
    for co in range(2):
        for x in range(4):
            at, to = x * 8 + co, (x * 2 + co) * 16
            rows_ref[to : to + 16, :] = (part_ref[at] + part_ref[at + 2]) + (part_ref[at + 4] + part_ref[at + 6])
    rows_ref[0:128] = rows_ref[0:128].T
    for zl in range(8):
        for zh in range(2):
            msg_ref[zh * 8 + zl] = rows_ref[pl.ds(zh * 64 + zl, 8, stride=8), :]


def norm_channels(values):
    center = values - jnp.mean(values, axis=0, keepdims=True)
    spread = jnp.mean(center * center, axis=0, keepdims=True)
    rstd = 1.0 / jnp.sqrt(spread + EPS)
    return center * rstd, rstd


def turn_kernel(home_ref, cot_ref, gate_ref, wout_ref, msg_ref, tri_ref, flat_ref, turn_ref):
    flat_ref[0:128] = home_ref[...].reshape(128, 128)
    for s in range(8):
        block = flat_ref[pl.ds(s, 16, stride=8), :]
        for a in range(8):
            turn_ref[a, :, s * 16 : (s + 1) * 16] = block[:, a * 16 : (a + 1) * 16]
    for a in range(8):
        flat_ref[pl.ds(a, 16, stride=8), :] = turn_ref[a]
    tri = flat_ref[0:128]
    tri_ref[...] = tri
    normed, rstd = norm_channels(tri)
    d_out = cot_ref[...].reshape(128, 128) * gate_ref[...]
    d_normed = dot(wout_ref[...], d_out, 1, 1)
    along = jnp.mean(d_normed * normed, axis=0, keepdims=True)
    flat_ref[0:128] = rstd * (d_normed - jnp.mean(d_normed, axis=0, keepdims=True) - normed * along)
    for a in range(8):
        block = flat_ref[pl.ds(a, 16, stride=8), :]
        for s in range(8):
            turn_ref[s, :, a * 16 : (a + 1) * 16] = block[:, s * 16 : (s + 1) * 16]
    for s in range(8):
        flat_ref[pl.ds(s, 16, stride=8), :] = turn_ref[s]
    msg_ref[...] = flat_ref[0:128].reshape(16, 8, 128)


def spread_kernel(msg_ref, out_ref, flat_ref, rows_ref):
    flat_ref[0:128] = msg_ref[...].reshape(128, 128)
    for zh in range(2):
        for s in range(8):
            to = zh * 64 + s * 8
            rows_ref[to : to + 8, :] = flat_ref[pl.ds(zh * 64 + s, 8, stride=8), :]
    turned = rows_ref[...].T
    for x in range(4):
        for co in range(2):
            block = turned[(x * 2 + co) * 16 : (x * 2 + co) * 16 + 16]
            for y in range(4):
                out_ref[(x * 4 + y) * 2 + co] = block


def back_kernel(dtri_ref, left_ref, right_ref, msg_ref, rows_ref, natural_ref, turn_ref):
    right = right_ref[...]
    total = jnp.zeros((128, 128), F32)
    for x in range(4):
        block = dtri_ref[x * 8 : (x + 1) * 8].reshape(128, 128)
        total += dot(block, left_ref[x * 128 : (x + 1) * 128], 1, 0)
        both = dot(block, right, 0, 0)
        rows_ref[x * 64 : (x + 1) * 64, :] = both[0:64, 0:64] + both[64:128, 64:128]
    for row, lane, at in column_blocks():
        natural_ref[at : at + 16, :] = total[row : row + 16, lane : lane + 64]
    for s in range(8):
        d_right = natural_ref[pl.ds(s, 32, stride=8), :]
        to = slice(s * 16, (s + 1) * 16)
        for x, co, zh in channel_blocks():
            lanes = slice(zh * 32 + co * 16, zh * 32 + co * 16 + 16)
            turn_ref[0, co, zh, x, :, to] = rows_ref[x * 64 + s * 8 : x * 64 + s * 8 + 8, lanes]
            turn_ref[1, co, zh, x, :, to] = d_right[x * 8 : (x + 1) * 8, lanes]
    for side in range(2):
        for x, co, zh in channel_blocks():
            msg_ref[pl.ds(zh * 64 + x * 2 + co, 8, stride=8), side, :] = turn_ref[side, co, zh, x]


def weights_kernel(
    msg_ref, factor_ref, normed_ref, tri_ref, cot_ref, gate_ref, wout_ref, weights_ref, dproj_ref, dpre_ref, out_ref
):
    normed = normed_ref[...]
    normed_tri, _ = norm_channels(tri_ref[...])
    gate = gate_ref[...]
    cot = cot_ref[...].reshape(128, 128)
    out_proj = dot(normed_tri, wout_ref[...], 0, 0)
    out_ref[...] = out_proj
    d_pre = cot * out_proj * gate * (1.0 - gate)
    dpre_ref[...] = d_pre
    weights_ref[512:640] = dot(normed, d_pre, 0, 0)
    weights_ref[640:768] = dot(normed_tri, cot * gate, 1, 0)
    for side in range(2):
        base = side * 256
        d_value = msg_ref[:, side, :] * factor_ref[base : base + 128]
        d_gate = d_value * factor_ref[base + 128 : base + 256]
        dproj_ref[base : base + 128] = d_gate
        dproj_ref[base + 128 : base + 256] = d_value
    d_win = dot(normed, dproj_ref[...], 0, 1)
    for f in range(4):
        weights_ref[f * 128 : (f + 1) * 128] = d_win[:, f * 128 : (f + 1) * 128]


def sum_kernel(scale, parts_ref, out_ref):
    total = jnp.sum(parts_ref[...], axis=0) * scale
    for i in range(out_ref.shape[0]):
        out_ref[i] = total


def leave_kernel(
    parts_ref, dproj_ref, dpre_ref, out_ref, gate_ref, pair_ref, win_ref, wgate_ref,
    dpair_hbm, upd_hbm, dwin_hbm, dwg_hbm, dwo_hbm, dpair_ref, upd_ref, sems
):
    pairs = [
        (parts_ref.at[pl.ds(f * 128, 128), :], dwin_hbm.at[:, pl.ds(f * 128, 128)]) for f in range(4)
    ]
    pairs += [(parts_ref.at[pl.ds(512, 128), :], dwg_hbm), (parts_ref.at[pl.ds(640, 128), :], dwo_hbm)]
    pairs += [(upd_ref, upd_hbm), (dpair_ref, dpair_hbm)]
    copies = [pltpu.make_async_copy(source, target, sems.at[i]) for i, (source, target) in enumerate(pairs)]
    for copy in copies[:6]:
        copy.start()
    upd_ref[...] = (gate_ref[...] * out_ref[...]).reshape(8, 16, 128)
    copies[6].start()
    normed, rstd = norm_rows(pair_ref[...].reshape(128, 128))
    d_normed = dot(dproj_ref[...], win_ref[...], 0, 1) + dot(dpre_ref[...], wgate_ref[...], 1, 1)
    along = jnp.mean(d_normed * normed, axis=1, keepdims=True)
    d_pair = rstd * (d_normed - jnp.mean(d_normed, axis=1, keepdims=True) - normed * along)
    dpair_ref[...] = d_pair.reshape(8, 16, 128)
    copies[7].start()
    for copy in copies:
        copy.wait()


def swap(values, axes):
    return lax.all_to_all(values, axes, split_axis=0, concat_axis=0, tiled=True)


def enter(pair, pair_mask, w_in, w_gate):
    lanes = pl.pallas_call(
        clear_kernel,
        out_shape=jax.ShapeDtypeStruct((8, 128), F32),
        out_specs=pl.BlockSpec(memory_space=pltpu.VMEM),
        cost_estimate=pl.CostEstimate(flops=10**10, bytes_accessed=2**25, transcendentals=0),
        compiler_params=pltpu.CompilerParams(vmem_limit_bytes=4 * 1024 * 1024),
    )()
    held = [(128, 2, 128), (512, 128), (128, 128), (128, 128)]
    return call(enter_kernel, held, [(8, 128)])(lanes, pair, pair_mask, w_in, w_gate)


def leave(*args):
    outs = [(8, 16, 128), (8, 16, 128), (128, 512), (128, 128), (128, 128)]
    return pl.pallas_call(
        leave_kernel,
        out_shape=[jax.ShapeDtypeStruct(s, F32) for s in outs],
        in_specs=[pl.BlockSpec(memory_space=pltpu.VMEM)] * len(args),
        out_specs=[pl.BlockSpec(memory_space=pl.ANY)] * len(outs),
        scratch_shapes=[pltpu.VMEM(outs[0], F32), pltpu.VMEM(outs[1], F32), pltpu.SemaphoreType.DMA((8,))],
        compiler_params=pltpu.CompilerParams(vmem_limit_bytes=32 * 1024 * 1024),
    )(*args)


def shards(pair, pair_mask, w_in, w_gate, w_out, cotangent):
    msg, factor, normed, gate = enter(pair, pair_mask, w_in, w_gate)
    msg = swap(msg, CHANNELS)
    part, left, right = call(
        triangle_kernel,
        [(32, 16, 128), (512, 128), (128, 128)],
        [(256, 64), (256, 64), (264, 64)],
    )(msg)
    part = swap(part, PLANE)
    (msg,) = call(home_kernel, [(16, 8, 128)], [(136, 128)])(part)
    msg = swap(msg, DEPTH)
    msg, tri = call(turn_kernel, [(16, 8, 128), (128, 128)], [(136, 128), (8, 16, 128)])(
        msg, cotangent, gate, w_out
    )
    msg = swap(msg, DEPTH)
    (d_tri,) = call(spread_kernel, [(32, 16, 128)], [(144, 128), (128, 128)])(msg)
    d_tri = swap(d_tri, PLANE)
    (msg,) = call(
        back_kernel,
        [(128, 2, 128)],
        [(256, 64), (264, 64), (2, 2, 2, 4, 8, 128)],
    )(d_tri, left, right)
    msg = swap(msg, CHANNELS)
    weights, d_proj, d_pre, out_proj = call(
        weights_kernel, [(768, 128), (512, 128), (128, 128), (128, 128)]
    )(msg, factor, normed, tri, cotangent, gate, w_out)
    parts = swap(weights.reshape(32, 24, 128), PLANE)
    (parts,) = call(lambda a, b: sum_kernel(1.0, a, b), [(16, 24, 128)])(parts)
    parts = swap(parts, DEPTH)
    scale = 1.0 / (pair.shape[0] * lax.axis_size(ROW))
    (parts,) = call(lambda a, b: sum_kernel(scale, a, b), [(32, 24, 128)])(parts)
    parts = swap(parts, PLANE)
    d_pair, update, d_win, d_wgate, d_wout = leave(
        parts.reshape(768, 128), d_proj, d_pre, out_proj, gate, pair, w_in, w_gate
    )
    return (update, d_pair, d_win, d_wgate, d_wout)


def solution(mesh):
    fine = Mesh(mesh.devices.reshape(4, 8, 4, 2, 2), ("x", "zl", "y", "zh", "co"))
    in_specs = (P(ROW, CH, None), P(ROW, CH), P(), P(), P(), P(ROW, CH, None))
    out_specs = (P(ROW, CH, None), P(ROW, CH, None), P(), P(), P())
    return jax.shard_map(shards, mesh=fine, in_specs=in_specs, out_specs=out_specs, check_vma=False)
```

```python
import jax
import jax.numpy as jnp
from jax import lax
from jax.experimental import pallas as pl
from jax.experimental.pallas import tpu as pltpu
from jax.sharding import Mesh, PartitionSpec as P

ROW = ("x", "zl")
CH = ("y", "zh", "co")
CHANNELS = ("zh", "zl", "x", "co")
PLANE = ("x", "y", "co")
DEPTH = ("zh", "zl")
SHARES = ("x", "co", "y")
F32 = jnp.float32
EPS = 1e-05


def dot(a, b, ca, cb):
    return lax.dot_general(
        a, b, (((ca,), (cb,)), ((), ())), precision=lax.Precision.HIGHEST, preferred_element_type=F32
    )


def call(body, outs, scratch=()):
    vmem = pl.BlockSpec(memory_space=pltpu.VMEM)

    def run(*args):
        return pl.pallas_call(
            body,
            out_shape=[jax.ShapeDtypeStruct(s, F32) for s in outs],
            in_specs=[vmem] * len(args),
            out_specs=[vmem] * len(outs),
            scratch_shapes=[pltpu.VMEM(s, F32) for s in scratch],
            compiler_params=pltpu.CompilerParams(vmem_limit_bytes=32 * 1024 * 1024),
        )(*args)

    return run


def norm_rows(values):
    center = values - jnp.mean(values, axis=1, keepdims=True)
    spread = jnp.mean(center * center, axis=1, keepdims=True)
    rstd = 1.0 / jnp.sqrt(spread + EPS)
    return center * rstd, rstd


def mask_lanes(mask_ref, lanes_ref):
    maskf = mask_ref[...].astype(F32)
    for ii in range(8):
        lanes_ref[0:1, ii * 16 : (ii + 1) * 16] = maskf[ii : ii + 1, :]
    return lanes_ref[0:1, :]


def clear_kernel(lanes_ref):
    lanes_ref[...] = jnp.zeros((8, 128), F32)


def enter_kernel(
    lanes_in, pair_ref, mask_ref, win_ref, wgate_ref, msg_ref, factor_ref, normed_ref, gate_ref, lanes_ref
):
    lanes_ref[...] = lanes_in[...]
    normed, _ = norm_rows(pair_ref[...].reshape(128, 128))
    normed_ref[...] = normed
    maskf = mask_lanes(mask_ref, lanes_ref)
    for side in range(2):
        base = side * 256
        proj = dot(win_ref[:, base : base + 256], normed, 0, 1)
        value = proj[128:256]
        sig = jax.nn.sigmoid(proj[0:128])
        masked = maskf * sig
        msg_ref[:, 0, side * 128 : (side + 1) * 128] = masked * value
        factor_ref[base : base + 128] = masked
        factor_ref[base + 128 : base + 256] = value * (1.0 - sig)
    gate_ref[...] = jax.nn.sigmoid(dot(normed, wgate_ref[...], 1, 0))


def column_blocks():
    return [
        ((y * 2 + co) * 16, zh * 64, y * 64 + zh * 32 + co * 16)
        for y in range(4) for co in range(2) for zh in range(2)
    ]


def channel_blocks():
    return [(x, co, zh) for x in range(4) for co in range(2) for zh in range(2)]


def triangle_kernel(msg_ref, part_ref, left_ref, right_ref, flat_ref, rows_ref, turn_ref, natural_ref):
    flat_ref[0, 0:128] = msg_ref[:, 0, 0:128]
    flat_ref[1, 0:128] = msg_ref[:, 0, 128:256]
    for x, co, zh in channel_blocks():
        source, lanes = pl.ds(zh * 64 + x * 2 + co, 8, stride=8), slice(zh * 32 + co * 16, zh * 32 + co * 16 + 16)
        left, right = flat_ref[0, source, :], flat_ref[1, source, :]
        for s in range(8):
            rows_ref[x * 64 + s * 8 : x * 64 + s * 8 + 8, lanes] = left[:, s * 16 : (s + 1) * 16]
            turn_ref[s * 32 + x * 8 : s * 32 + x * 8 + 8, lanes] = right[:, s * 16 : (s + 1) * 16]
    for s in range(8):
        natural_ref[pl.ds(s, 32, stride=8), :] = turn_ref[s * 32 : (s + 1) * 32, :]
    for row, lane, at in column_blocks():
        right_ref[row : row + 16, lane : lane + 64] = natural_ref[at : at + 16, :]
    left_ref[...] = jnp.zeros((512, 128), F32)
    for x in range(4):
        block = rows_ref[x * 64 : (x + 1) * 64, :]
        left_ref[x * 128 : x * 128 + 64, 0:64] = block
        left_ref[x * 128 + 64 : x * 128 + 128, 64:128] = block
    part = dot(right_ref[...], left_ref[...], 1, 1)
    for x in range(4):
        part_ref[x * 8 : (x + 1) * 8] = part[:, x * 128 : (x + 1) * 128].reshape(8, 16, 128)


def home_kernel(part_ref, msg_ref, rows_ref):
    for co in range(2):
        for x in range(4):
            at, to = x * 8 + co, (x * 2 + co) * 16
            rows_ref[to : to + 16, :] = (part_ref[at] + part_ref[at + 2]) + (part_ref[at + 4] + part_ref[at + 6])
    rows_ref[0:128] = rows_ref[0:128].T
    for zl in range(8):
        for zh in range(2):
            msg_ref[zh * 8 + zl] = rows_ref[pl.ds(zh * 64 + zl, 8, stride=8), :]


def norm_channels(values):
    center = values - jnp.mean(values, axis=0, keepdims=True)
    spread = jnp.mean(center * center, axis=0, keepdims=True)
    rstd = 1.0 / jnp.sqrt(spread + EPS)
    return center * rstd, rstd


def turn_kernel(home_ref, cot_ref, gate_ref, wout_ref, msg_ref, tri_ref, flat_ref, turn_ref):
    flat_ref[0:128] = home_ref[...].reshape(128, 128)
    for s in range(8):
        block = flat_ref[pl.ds(s, 16, stride=8), :]
        for a in range(8):
            turn_ref[a, :, s * 16 : (s + 1) * 16] = block[:, a * 16 : (a + 1) * 16]
    for a in range(8):
        flat_ref[pl.ds(a, 16, stride=8), :] = turn_ref[a]
    tri = flat_ref[0:128]
    tri_ref[...] = tri
    normed, rstd = norm_channels(tri)
    d_out = cot_ref[...].reshape(128, 128) * gate_ref[...]
    d_normed = dot(wout_ref[...], d_out, 1, 1)
    along = jnp.mean(d_normed * normed, axis=0, keepdims=True)
    flat_ref[0:128] = rstd * (d_normed - jnp.mean(d_normed, axis=0, keepdims=True) - normed * along)
    for a in range(8):
        block = flat_ref[pl.ds(a, 16, stride=8), :]
        for s in range(8):
            turn_ref[s, :, a * 16 : (a + 1) * 16] = block[:, s * 16 : (s + 1) * 16]
    for s in range(8):
        flat_ref[pl.ds(s, 16, stride=8), :] = turn_ref[s]
    msg_ref[...] = flat_ref[0:128].reshape(16, 8, 128)


def spread_kernel(msg_ref, out_ref, flat_ref, rows_ref):
    flat_ref[0:128] = msg_ref[...].reshape(128, 128)
    for zh in range(2):
        for s in range(8):
            to = zh * 64 + s * 8
            rows_ref[to : to + 8, :] = flat_ref[pl.ds(zh * 64 + s, 8, stride=8), :]
    turned = rows_ref[...].T
    for x in range(4):
        for co in range(2):
            block = turned[(x * 2 + co) * 16 : (x * 2 + co) * 16 + 16]
            for y in range(4):
                out_ref[(x * 4 + y) * 2 + co] = block


def back_kernel(dtri_ref, left_ref, right_ref, msg_ref, flat_ref, rows_ref, natural_ref, turn_ref):
    right = right_ref[...]
    total = jnp.zeros((128, 128), F32)
    for x in range(4):
        block = dtri_ref[x * 8 : (x + 1) * 8].reshape(128, 128)
        total += dot(block, left_ref[x * 128 : (x + 1) * 128], 1, 0)
        both = dot(block, right, 0, 0)
        rows_ref[x * 64 : (x + 1) * 64, :] = both[0:64, 0:64] + both[64:128, 64:128]
    for row, lane, at in column_blocks():
        natural_ref[at : at + 16, :] = total[row : row + 16, lane : lane + 64]
    for s in range(8):
        d_right = natural_ref[pl.ds(s, 32, stride=8), :]
        to = slice(s * 16, (s + 1) * 16)
        for x, co, zh in channel_blocks():
            lanes = slice(zh * 32 + co * 16, zh * 32 + co * 16 + 16)
            turn_ref[0, co, zh, x, :, to] = rows_ref[x * 64 + s * 8 : x * 64 + s * 8 + 8, lanes]
            turn_ref[1, co, zh, x, :, to] = d_right[x * 8 : (x + 1) * 8, lanes]
    for side in range(2):
        for x, co, zh in channel_blocks():
            flat_ref[side, pl.ds(zh * 64 + x * 2 + co, 8, stride=8), :] = turn_ref[side, co, zh, x]
        msg_ref[:, 0, side * 128 : (side + 1) * 128] = flat_ref[side, 0:128]


def weights_kernel(
    msg_ref, factor_ref, normed_ref, tri_ref, cot_ref, gate_ref, wout_ref, weights_ref, dproj_ref, dpre_ref, out_ref
):
    normed = normed_ref[...]
    normed_tri, _ = norm_channels(tri_ref[...])
    gate = gate_ref[...]
    cot = cot_ref[...].reshape(128, 128)
    out_proj = dot(normed_tri, wout_ref[...], 0, 0)
    out_ref[...] = out_proj
    d_pre = cot * out_proj * gate * (1.0 - gate)
    dpre_ref[...] = d_pre
    weights_ref[512:640] = dot(normed, d_pre, 0, 0)
    weights_ref[640:768] = dot(normed_tri, cot * gate, 1, 0)
    for side in range(2):
        base = side * 256
        d_value = msg_ref[:, 0, side * 128 : (side + 1) * 128] * factor_ref[base : base + 128]
        d_gate = d_value * factor_ref[base + 128 : base + 256]
        dproj_ref[base : base + 128] = d_gate
        dproj_ref[base + 128 : base + 256] = d_value
    d_win = dot(normed, dproj_ref[...], 0, 1)
    for f in range(4):
        weights_ref[f * 128 : (f + 1) * 128] = d_win[:, f * 128 : (f + 1) * 128]


def sum_kernel(scale, parts_ref, out_ref):
    total = jnp.sum(parts_ref[...], axis=0) * scale
    for i in range(out_ref.shape[0]):
        out_ref[i] = total


def leave_kernel(
    parts_ref, dproj_ref, dpre_ref, out_ref, gate_ref, pair_ref, win_ref, wgate_ref,
    dpair_hbm, upd_hbm, dwin_hbm, dwg_hbm, dwo_hbm, dpair_ref, upd_ref, sems
):
    pairs = [
        (parts_ref.at[pl.ds(f * 128, 128), :], dwin_hbm.at[:, pl.ds(f * 128, 128)]) for f in range(4)
    ]
    pairs += [(parts_ref.at[pl.ds(512, 128), :], dwg_hbm), (parts_ref.at[pl.ds(640, 128), :], dwo_hbm)]
    pairs += [(upd_ref, upd_hbm), (dpair_ref, dpair_hbm)]
    copies = [pltpu.make_async_copy(source, target, sems.at[i]) for i, (source, target) in enumerate(pairs)]
    for copy in copies[:6]:
        copy.start()
    upd_ref[...] = (gate_ref[...] * out_ref[...]).reshape(8, 16, 128)
    copies[6].start()
    normed, rstd = norm_rows(pair_ref[...].reshape(128, 128))
    d_normed = dot(dproj_ref[...], win_ref[...], 0, 1) + dot(dpre_ref[...], wgate_ref[...], 1, 1)
    along = jnp.mean(d_normed * normed, axis=1, keepdims=True)
    d_pair = rstd * (d_normed - jnp.mean(d_normed, axis=1, keepdims=True) - normed * along)
    dpair_ref[...] = d_pair.reshape(8, 16, 128)
    copies[7].start()
    for copy in copies:
        copy.wait()


def swap(values, axes):
    return lax.all_to_all(values, axes, split_axis=0, concat_axis=0, tiled=True)


def enter(pair, pair_mask, w_in, w_gate):
    lanes = pl.pallas_call(
        clear_kernel,
        out_shape=jax.ShapeDtypeStruct((8, 128), F32),
        out_specs=pl.BlockSpec(memory_space=pltpu.VMEM),
        cost_estimate=pl.CostEstimate(flops=10**10, bytes_accessed=2**25, transcendentals=0),
        compiler_params=pltpu.CompilerParams(vmem_limit_bytes=4 * 1024 * 1024),
    )()
    held = [(128, 1, 256), (512, 128), (128, 128), (128, 128)]
    return call(enter_kernel, held, [(8, 128)])(lanes, pair, pair_mask, w_in, w_gate)


def leave(*args):
    outs = [(8, 16, 128), (8, 16, 128), (128, 512), (128, 128), (128, 128)]
    return pl.pallas_call(
        leave_kernel,
        out_shape=[jax.ShapeDtypeStruct(s, F32) for s in outs],
        in_specs=[pl.BlockSpec(memory_space=pltpu.VMEM)] * len(args),
        out_specs=[pl.BlockSpec(memory_space=pl.ANY)] * len(outs),
        scratch_shapes=[pltpu.VMEM(outs[0], F32), pltpu.VMEM(outs[1], F32), pltpu.SemaphoreType.DMA((8,))],
        compiler_params=pltpu.CompilerParams(vmem_limit_bytes=32 * 1024 * 1024),
    )(*args)


def shards(pair, pair_mask, w_in, w_gate, w_out, cotangent):
    msg, factor, normed, gate = enter(pair, pair_mask, w_in, w_gate)
    msg = swap(msg, CHANNELS)
    part, left, right = call(
        triangle_kernel,
        [(32, 16, 128), (512, 128), (128, 128)],
        [(2, 144, 128), (256, 64), (256, 64), (264, 64)],
    )(msg)
    part = swap(part, PLANE)
    (msg,) = call(home_kernel, [(16, 8, 128)], [(136, 128)])(part)
    msg = swap(msg, DEPTH)
    msg, tri = call(turn_kernel, [(16, 8, 128), (128, 128)], [(136, 128), (8, 16, 128)])(
        msg, cotangent, gate, w_out
    )
    msg = swap(msg, DEPTH)
    (d_tri,) = call(spread_kernel, [(32, 16, 128)], [(144, 128), (128, 128)])(msg)
    d_tri = swap(d_tri, PLANE)
    (msg,) = call(
        back_kernel,
        [(128, 1, 256)],
        [(2, 144, 128), (256, 64), (264, 64), (2, 2, 2, 4, 8, 128)],
    )(d_tri, left, right)
    msg = swap(msg, CHANNELS)
    weights, d_proj, d_pre, out_proj = call(
        weights_kernel, [(768, 128), (512, 128), (128, 128), (128, 128)]
    )(msg, factor, normed, tri, cotangent, gate, w_out)
    parts = swap(weights.reshape(32, 24, 128), SHARES)
    (parts,) = call(lambda a, b: sum_kernel(1.0, a, b), [(16, 24, 128)])(parts)
    parts = swap(parts, DEPTH)
    scale = 1.0 / (pair.shape[0] * lax.axis_size(ROW))
    (parts,) = call(lambda a, b: sum_kernel(scale, a, b), [(32, 24, 128)])(parts)
    parts = swap(parts, SHARES)
    d_pair, update, d_win, d_wgate, d_wout = leave(
        parts.reshape(768, 128), d_proj, d_pre, out_proj, gate, pair, w_in, w_gate
    )
    return (update, d_pair, d_win, d_wgate, d_wout)


def solution(mesh):
    fine = Mesh(mesh.devices.reshape(4, 8, 4, 2, 2), ("x", "zl", "y", "zh", "co"))
    in_specs = (P(ROW, CH, None), P(ROW, CH), P(), P(), P(), P(ROW, CH, None))
    out_specs = (P(ROW, CH, None), P(ROW, CH, None), P(), P(), P())
    return jax.shard_map(shards, mesh=fine, in_specs=in_specs, out_specs=out_specs, check_vma=False)
```
